256 devices in a mesh: replica: 8 (over z_hi, core), fsdp: 32 (over z_lo, y, x).
Axes of the slice: x: 4, y: 4, z: 8 (z_hi: 4, z_lo: 2; z = z_hi * 2 + z_lo), core: 2. Of those that a mesh axis runs over, the one named last changes fastest.
Arguments:
- out_grad: bfloat16 [8, 16384, 8192], P('replica', 'fsdp'), may hold values from -8 to 8
- hidden_act: bfloat16 [8, 16384, 448], P('replica', 'fsdp'), may hold values from -40 to 40
- inner_params: float32 [8, 448, 8192], P('replica', None, 'fsdp'), may hold values from -6 to 6
- first_moment: float32 [8, 448, 8192], P('replica', None, 'fsdp'), may hold values from -4 to 4
- second_moment: float32 [8, 448, 8192], P('replica', None, 'fsdp'), may hold values from 0.05 to 2
- anchor: float32 [448, 8192], P(None, 'fsdp'), may hold values from -6 to 6
- outer_velocity: float32 [448, 8192], P(None, 'fsdp'), may hold values from -4 to 4
Outputs:
- new_first: float32 [8, 448, 8192], P('replica', None, 'fsdp')
- new_second: float32 [8, 448, 8192], P('replica', None, 'fsdp')
- new_anchor: float32 [448, 8192], P(None, 'fsdp')
- new_velocity: float32 [448, 8192], P(None, 'fsdp')
The draws below stay inside these ranges and needn't reach their ends.
All inputs are finite; a program needn't handle non-finite values.
Results may differ from the reference program's by a relative error of at most 0.0003.
Values may be sent and summed in bfloat16 or wider, within the bound.
A program may use at most 128 MiB of HBM per device.

```python
import math
import jax
import jax.numpy as jnp
from jax import lax

D = 8192
H = 448
TOKENS = 16384
REPLICAS = 8


def draw_out_grad(key, part):
    key = jax.random.fold_in(key, 11)
    key_rows, key_cols, key_base, key_level, key_order = jax.random.split(key, 5)
    row_scale = jnp.exp(jax.random.uniform(key_rows, (REPLICAS, TOKENS, 1), jnp.float32, 0.0, math.log(10.0)))
    col_scale = jnp.exp(jax.random.uniform(key_cols, (1, 1, D), jnp.float32, 0.0, math.log(10.0)))
    position = jnp.arange(D, dtype=jnp.float32)[None, None, :] / D
    order = jax.random.permutation(key_order, REPLICAS)
    spread = jax.random.uniform(key_level, (REPLICAS,), jnp.float32, 0.0, 1.0)
    quiet = jnp.exp(math.log(0.15) + spread * math.log(0.35 / 0.15))
    loud = jnp.exp(math.log(3.0) + spread * math.log(8.0 / 3.0))
    level = jnp.where(order < REPLICAS // 2, quiet, loud)
    col_power = 99.0 / (2.0 * math.log(10.0))
    base = jnp.clip(jax.random.normal(key_base, (REPLICAS, TOKENS, D), jnp.float32), -4.0, 4.0)
    rising = jnp.exp(position * math.log(3.0))
    expected = TOKENS * col_power * col_power * col_power * (8.0 / math.log(9.0))
    factor = level / math.sqrt(expected)
    return (base * row_scale * col_scale * rising * factor[:, None, None]).astype(jnp.bfloat16)


def draw_hidden_act(key, part):
    key = jax.random.fold_in(key, 23)
    key_cols, key_base = jax.random.split(key, 2)
    col_scale = jnp.exp(jax.random.uniform(key_cols, (1, 1, H), jnp.float32, 0.0, math.log(10.0)))
    base = jnp.clip(jax.random.normal(key_base, (REPLICAS, TOKENS, H), jnp.float32), -4.0, 4.0)
    return (base * col_scale).astype(jnp.bfloat16)


def block_levels(rng, dims, cuts, least, largest):
    factor_of, own = 1.0, jax.random.fold_in(rng, 6)
    for dim, blocks in cuts:
        steps = jnp.exp(jax.random.uniform(jax.random.fold_in(own, dim), (blocks,), jnp.float32, least / len(cuts), largest / len(cuts)))
        factor_of = factor_of * jnp.repeat(steps, dims[dim] // blocks).reshape([-1 if axis == dim else 1 for axis in range(len(dims))])
    return factor_of


def centred(stream_key, dims, width, reach, shards=(), kind=jnp.bfloat16):
    array = jax.random.normal(stream_key, dims, jnp.float32) * width
    if len(shards) > 0:
        array = block_levels(stream_key, dims, shards, -0.22, 0.18) * array
    return jnp.clip(array, min=-reach, max=reach).astype(kind)


def setup_inputs(seed: int = 0) -> dict:
    arg_keys = jax.random.split(jax.random.key(seed), 8)
    out_grad = draw_out_grad(jax.random.fold_in(arg_keys[7], 71), 0)
    hidden_act = draw_hidden_act(jax.random.fold_in(arg_keys[7], 71), 0)
    inner_params = centred(arg_keys[2], (REPLICAS, H, D), 1.0, 6.0, ((0, 8), (2, 32)), jnp.float32)
    first_moment = centred(arg_keys[3], (REPLICAS, H, D), 0.5, 4.0, ((0, 8), (2, 32)), jnp.float32)
    second_moment = jnp.clip(jnp.exp(math.log(2.0) - 3.6888794 * jax.random.uniform(arg_keys[4], (REPLICAS, H, D), jnp.float32) ** block_levels(arg_keys[4], (REPLICAS, H, D), ((0, 8), (2, 32)), -0.2, 0.2)), 0.05, 2.0)
    anchor = centred(arg_keys[5], (H, D), 1.0, 6.0, ((1, 32),), jnp.float32)
    outer_velocity = centred(arg_keys[6], (H, D), 0.5, 4.0, ((1, 32),), jnp.float32)
    return dict(out_grad=out_grad, hidden_act=hidden_act, inner_params=inner_params, first_moment=first_moment, second_moment=second_moment, anchor=anchor, outer_velocity=outer_velocity)


beta_one = 0.9
beta_two = 0.95
inner_rate = 0.1
decay_rate = 0.1
adam_eps = 1e-08
clip_eps = 1e-06
outer_rate = 0.7
outer_mom = 0.9
bias_one = 1.0 - 0.9 ** 50
bias_two = 1.0 - 0.95 ** 50

def reference(out_grad, hidden_act, inner_params, first_moment, second_moment, anchor, outer_velocity):
    firsts = []
    seconds = []
    summed = jnp.zeros_like(anchor)
    for replica_id in range(REPLICAS):
        gradient_raw = jnp.dot(hidden_act[replica_id].T, out_grad[replica_id], preferred_element_type=jnp.float32)
        mean_square = jnp.mean(gradient_raw * gradient_raw)
        clip_factor = jnp.minimum(1.0, lax.rsqrt(mean_square + clip_eps))
        gradient = gradient_raw * clip_factor
        moment = beta_one * first_moment[replica_id] + (1.0 - beta_one) * gradient
        second = beta_two * second_moment[replica_id] + (1.0 - beta_two) * gradient * gradient
        params = inner_params[replica_id]
        stepped = params - inner_rate * (moment / bias_one / (jnp.sqrt(second / bias_two) + adam_eps) + decay_rate * params)
        summed = summed + (anchor - stepped)
        firsts.append(moment)
        seconds.append(second)
    pseudo_grad = summed / REPLICAS
    velocity = outer_mom * outer_velocity + pseudo_grad
    new_anchor = anchor - outer_rate * (pseudo_grad + outer_mom * velocity)
    return (jnp.stack(firsts), jnp.stack(seconds), new_anchor, velocity)
```

```python
import functools

import jax
import jax.numpy as jnp
from jax import lax
from jax.experimental import pallas as pl
from jax.experimental.pallas import tpu as pltpu
from jax.sharding import PartitionSpec as P

beta_one = 0.9
beta_two = 0.95
inner_rate = 0.1
decay_rate = 0.1
adam_eps = 1e-08
clip_eps = 1e-06
outer_rate = 0.7
outer_mom = 0.9
bias_one = 1.0 - 0.9**50
bias_two = 1.0 - 0.95**50

MESH = pl.DeviceIdType.MESH
LANES = 128
PAD = 16
REACH = 86.0
RING = 4
ITEMS = 8


def column_scale(values):
    largest = jnp.max(jnp.abs(values), axis=0, keepdims=True)
    return (largest * 1.01 + 1e-30).astype(jnp.bfloat16).astype(jnp.float32)


def encode(message, parts):
    rows = parts[0].shape[0]
    bounds = []
    for n, values in enumerate(parts):
        bound = column_scale(values)
        message[n * rows : (n + 1) * rows, :] = jnp.exp(values * (REACH / bound)).astype(jnp.bfloat16)
        bounds.append(bound)
    base = len(parts) * rows
    if len(parts) == 1:
        block = jnp.broadcast_to(bounds[0], (PAD, LANES))
    else:
        upper = lax.broadcasted_iota(jnp.int32, (PAD, LANES), 0) < PAD // 2
        block = jnp.where(upper, bounds[0], bounds[1])
    message[base : base + PAD, :] = block.astype(jnp.bfloat16)


def decode(message, count, which, rows):
    base = count * rows
    block = message[base : base + PAD, :].astype(jnp.float32)
    row = which * (PAD // 2) if count > 1 else 0
    bound = block[row : row + 1, :] * (1.0 / REACH)
    return jnp.log(message[which * rows : (which + 1) * rows, :].astype(jnp.float32)) * bound


def kernel(
    cotangent, activations, inner, first, second, anchor,
    gradient_out, pseudo_out,
    cot, act_t, inner_v, first_v, second_v, anchor_v,
    partial, send_a, recv_a, send_b, recv_b, send_z, recv_z,
    norm_send, norm_recv, half_send, half_recv, quarter_send, quarter_recv,
    whole_send, whole_recv, twin_recv, half_sum,
    cot_sem, state_sem, sa_sem, ra_sem, sb_sem, rb_sem, sz_sem, rz_sem,
    ns_sem, nr_sem, hs_sem, hr_sem, qs_sem, qr_sem, ws_sem, wr_sem, ts_sem, tr_sem,
):
    hidden, tokens = act_t.shape
    rows = hidden // 2
    width = 2 * LANES
    me = lax.axis_index("fsdp")
    rep = lax.axis_index("replica")
    x = me % RING
    y = (me // RING) % RING
    z = me // (RING * RING)
    core = rep % 2
    zh = rep // 2

    def at(px, py, pz):
        return {"fsdp": pz * (RING * RING) + py * RING + px}

    def twin(pzh, pcore):
        return {"replica": pzh * 2 + pcore}

    def along(axis, step):
        if axis == 0:
            return at((x + step) % RING, y, z)
        return at(x, (y + step) % RING, z)

    here = (x, y)
    pair = at(x, y, 1 - z)
    peers = [along(axis, step) for axis in (0, 1) for step in (1, 2, 3)] + [pair]
    twins = [twin((zh + step) % RING, core) for step in (1, 2, 3)]
    mate = twin(zh, 1 - core)

    halves = cotangent.shape[1] // 2
    loads = []
    for k in range(2):
        zz = (1 - z) if k == 0 else z
        loads.append(pltpu.make_async_copy(
            cotangent.at[:, pl.ds(pl.multiple_of(zz * halves, halves), halves)], cot.at[k], cot_sem.at[k]))
        loads[k].start()
    states = []
    for n, (src, dst) in enumerate(((inner, inner_v), (first, first_v), (second, second_v), (anchor, anchor_v))):
        states.append(pltpu.make_async_copy(src, dst, state_sem.at[n]))
        states[n].start()

    barrier = pltpu.get_barrier_semaphore()
    everyone = peers + twins + [mate]
    for device in everyone:
        pl.semaphore_signal(barrier, inc=1, device_id=device, device_id_type=MESH)

    act_t[...] = activations[...].T
    loads[0].wait()
    pl.semaphore_wait(barrier, len(everyone))

    def copy_a(s, axis, i, way):
        return pltpu.make_async_remote_copy(
            src_ref=send_a.at[s, i, way], dst_ref=recv_a.at[s, i, way],
            send_sem=sa_sem.at[s, i, way], recv_sem=ra_sem.at[s, i, way],
            device_id=along(axis, 1 if way == 0 else 3), device_id_type=MESH)

    def copy_b(s, axis, i, way):
        return pltpu.make_async_remote_copy(
            src_ref=send_b.at[s, i, way], dst_ref=recv_b.at[s, i, way],
            send_sem=sb_sem.at[s, i, way], recv_sem=rb_sem.at[s, i, way],
            device_id=along(axis, 1 if way == 0 else 3), device_id_type=MESH)

    def copy_z(s):
        return pltpu.make_async_remote_copy(
            src_ref=send_z.at[s], dst_ref=recv_z.at[s], send_sem=sz_sem.at[s], recv_sem=rz_sem.at[s],
            device_id=pair, device_id_type=MESH)

    def product(s, i, t):
        k, w = i // RING, i % RING
        chunk = w * RING + t if s == 0 else t * RING + w
        columns = pl.ds(pl.multiple_of(chunk * width, width), width)
        return jnp.dot(act_t[s * rows : (s + 1) * rows, :], cot[k, :, columns], preferred_element_type=jnp.float32)

    def round_a(s, axis, i, own):
        opposite = own(s, i, (here[axis] + 2) % RING)
        encode(send_a.at[s, i, 0], [opposite[:, :LANES]])
        copy_a(s, axis, i, 0).start()
        encode(send_a.at[s, i, 1], [opposite[:, LANES:]])
        copy_a(s, axis, i, 1).start()

    def round_b(s, axis, i, own):
        for way in range(2):
            value = own(s, i, (here[axis] + (1 if way == 0 else 3)) % RING)
            copy_a(s, axis, i, way).wait_recv()
            arrived = decode(recv_a.at[s, i, way], 1, 0, rows)
            left, right = value[:, :LANES], value[:, LANES:]
            if way == 0:
                left = left + arrived
            else:
                right = right + arrived
            encode(send_b.at[s, i, way], [left, right])
            copy_b(s, axis, i, way).start()

    def round_c(s, axis, i, own):
        value = own(s, i, here[axis])
        for way in range(2):
            copy_b(s, axis, i, way).wait_recv()
        parts = []
        for n in range(2):
            parts.append(value[:, n * LANES : (n + 1) * LANES]
                         + decode(recv_b.at[s, i, 0], 2, n, rows) + decode(recv_b.at[s, i, 1], 2, n, rows))
        for way in range(2):
            copy_a(s, axis, i, way).wait_send()
            copy_b(s, axis, i, way).wait_send()
        return parts

    def summed(s, i, t):
        return partial[s, i - ITEMS, t]

    def finish_other(s):
        parts = round_c(s, 1 - s, ITEMS, summed)
        encode(send_z.at[s], parts)
        copy_z(s).start()

    @pl.loop(0, ITEMS + 2)
    def _(step):
        @pl.when(step == RING)
        def _():
            pltpu.make_async_copy(
                cotangent.at[:, pl.ds(pl.multiple_of(z * halves, halves), halves)], cot.at[1], cot_sem.at[1]).wait()

        @pl.when(step < ITEMS)
        def _():
            for s in range(2):
                round_a(s, s, step, product)

        @pl.when(jnp.logical_and(step >= 1, step < ITEMS + 1))
        def _():
            for s in range(2):
                round_b(s, s, step - 1, product)

        @pl.when(step >= 2)
        def _():
            i = step - 2
            for s in range(2):
                parts = round_c(s, s, i, product)
                for n in range(2):
                    partial[s, i // RING, i % RING, :, n * LANES : (n + 1) * LANES] = parts[n]

        @pl.when(step == RING + 2)
        def _():
            for s in range(2):
                round_a(s, 1 - s, ITEMS, summed)

        @pl.when(step == RING + 3)
        def _():
            for s in range(2):
                round_b(s, 1 - s, ITEMS, summed)

        @pl.when(step == RING + 4)
        def _():
            for s in range(2):
                finish_other(s)

    last = ITEMS + 1
    for s in range(2):
        round_a(s, 1 - s, last, summed)
    for s in range(2):
        round_b(s, 1 - s, last, summed)
    total = jnp.zeros((8, LANES), jnp.float32)
    for s in range(2):
        parts = round_c(s, 1 - s, last, summed)
        copy_z(s).wait_recv()
        for n in range(2):
            value = parts[n] + decode(recv_z.at[s], 2, n, rows)
            gradient_out[s * rows : (s + 1) * rows, n * LANES : (n + 1) * LANES] = value
            total = total + jnp.sum((value * value).reshape(rows // 8, 8, LANES), axis=0)
    for s in range(2):
        copy_z(s).wait_send()

    slot = 0
    for phase in range(3):
        group = peers[3 * phase : 3 * phase + 3]
        norm_send[phase] = total
        copies = [
            pltpu.make_async_remote_copy(
                src_ref=norm_send.at[phase], dst_ref=norm_recv.at[slot + n],
                send_sem=ns_sem.at[slot + n], recv_sem=nr_sem.at[slot + n],
                device_id=device, device_id_type=MESH)
            for n, device in enumerate(group)
        ]
        for copy in copies:
            copy.start()
        if phase == 0:
            for state in states:
                state.wait()
        for copy in copies:
            copy.wait()
        for n in range(len(group)):
            total = total + norm_recv[slot + n]
        slot += len(group)

    mean_square = jnp.sum(total) / (hidden * cotangent.shape[1])
    clip_factor = jnp.minimum(1.0, lax.rsqrt(jnp.full((1, LANES), mean_square + clip_eps, jnp.float32)))

    def difference(columns):
        gradient = gradient_out[:, columns] * clip_factor
        gradient_out[:, columns] = gradient
        moment = beta_one * first_v[:, columns] + (1.0 - beta_one) * gradient
        square = beta_two * second_v[:, columns] + (1.0 - beta_two) * gradient * gradient
        params = inner_v[:, columns]
        stepped = params - inner_rate * (
            moment / bias_one / (jnp.sqrt(square / bias_two) + adam_eps) + decay_rate * params)
        return anchor_v[:, columns] - stepped

    given = pl.ds(pl.multiple_of((1 - core) * LANES, LANES), LANES)
    kept = pl.ds(pl.multiple_of(core * LANES, LANES), LANES)
    encode(half_send, [difference(given)])
    to_mate = pltpu.make_async_remote_copy(
        src_ref=half_send, dst_ref=half_recv, send_sem=hs_sem, recv_sem=hr_sem, device_id=mate, device_id_type=MESH)
    to_mate.start()
    half_sum[...] = difference(kept)
    to_mate.wait()
    half_sum[...] = half_sum[...] + decode(half_recv, 1, 0, hidden)

    piece = hidden // RING
    def rows_of(q):
        return pl.ds(pl.multiple_of(q * piece, piece), piece)

    copies = []
    for n in range(3):
        encode(quarter_send.at[n], [half_sum[rows_of((zh + n + 1) % RING), :]])
        copies.append(pltpu.make_async_remote_copy(
            src_ref=quarter_send.at[n], dst_ref=quarter_recv.at[n], send_sem=qs_sem.at[n], recv_sem=qr_sem.at[n],
            device_id=twins[n], device_id_type=MESH))
        copies[n].start()
    for copy in copies:
        copy.wait()
    mine = half_sum[rows_of(zh), :]
    for n in range(3):
        mine = mine + decode(quarter_recv.at[n], 1, 0, piece)

    encode(whole_send, [mine])
    spread = []
    for n in range(3):
        spread.append(pltpu.make_async_remote_copy(
            src_ref=whole_send, dst_ref=whole_recv.at[n], send_sem=ws_sem.at[n], recv_sem=wr_sem.at[n],
            device_id=twins[n], device_id_type=MESH))
        spread[n].start()

    def forward(source, n):
        return pltpu.make_async_remote_copy(
            src_ref=source, dst_ref=twin_recv.at[n], send_sem=ts_sem.at[n], recv_sem=tr_sem.at[n],
            device_id=mate, device_id_type=MESH)

    passed = [forward(whole_send, 3)]
    passed[0].start()
    pseudo_out[rows_of(zh), kept] = decode(whole_send, 1, 0, piece)
    for n in range(3):
        spread[n].wait_recv()
        passed.append(forward(whole_recv.at[n], n))
        passed[-1].start()
        pseudo_out[rows_of((zh + 3 - n) % RING), kept] = decode(whole_recv.at[n], 1, 0, piece)
    passed[0].wait_recv()
    pseudo_out[rows_of(zh), given] = decode(twin_recv.at[3], 1, 0, piece)
    for n in range(3):
        passed[n + 1].wait_recv()
        pseudo_out[rows_of((zh + 3 - n) % RING), given] = decode(twin_recv.at[n], 1, 0, piece)
    for copy in spread + passed:
        copy.wait_send()


def shards(out_grad, hidden_act, inner_params, first_moment, second_moment, anchor, outer_velocity):
    cotangent, activations = out_grad[0], hidden_act[0]
    tokens, hidden = activations.shape
    columns = anchor.shape[1]
    replicas = lax.axis_size("replica")
    rows = hidden // 2
    piece = hidden // RING
    bf16, f32 = jnp.bfloat16, jnp.float32
    vmem, dma = pltpu.VMEM, pltpu.SemaphoreType.DMA
    count = ITEMS + 2
    anywhere = pl.BlockSpec(memory_space=pl.ANY)
    local = pl.BlockSpec(memory_space=pltpu.VMEM)
    gradient, pseudo = pl.pallas_call(
        kernel,
        out_shape=(jax.ShapeDtypeStruct((hidden, columns), f32),) * 2,
        in_specs=[anywhere, local] + [anywhere] * 4,
        out_specs=(local, local),
        scratch_shapes=[
            vmem((2, tokens, cotangent.shape[1] // 2), bf16),
            vmem((hidden, tokens), bf16),
            *[vmem((hidden, columns), f32)] * 4,
            vmem((2, 2, RING, rows, columns), f32),
            vmem((2, count, 2, rows + PAD, LANES), bf16),
            vmem((2, count, 2, rows + PAD, LANES), bf16),
            vmem((2, count, 2, 2 * rows + PAD, LANES), bf16),
            vmem((2, count, 2, 2 * rows + PAD, LANES), bf16),
            vmem((2, 2 * rows + PAD, LANES), bf16),
            vmem((2, 2 * rows + PAD, LANES), bf16),
            vmem((3, 8, LANES), f32),
            vmem((7, 8, LANES), f32),
            vmem((hidden + PAD, LANES), bf16),
            vmem((hidden + PAD, LANES), bf16),
            vmem((3, piece + PAD, LANES), bf16),
            vmem((3, piece + PAD, LANES), bf16),
            vmem((piece + PAD, LANES), bf16),
            vmem((3, piece + PAD, LANES), bf16),
            vmem((4, piece + PAD, LANES), bf16),
            vmem((hidden, LANES), f32),
            dma((2,)), dma((4,)),
            dma((2, count, 2)), dma((2, count, 2)), dma((2, count, 2)), dma((2, count, 2)),
            dma((2,)), dma((2,)), dma((7,)), dma((7,)), dma, dma,
            dma((3,)), dma((3,)), dma((3,)), dma((3,)), dma((4,)), dma((4,)),
        ],
        compiler_params=pltpu.CompilerParams(
            collective_id=0, has_side_effects=True, vmem_limit_bytes=52 * 1024 * 1024),
        cost_estimate=pl.CostEstimate(
            flops=2 * tokens * hidden * cotangent.shape[1], bytes_accessed=12_000_000, transcendentals=8_000_000),
    )(cotangent, activations, inner_params[0], first_moment[0], second_moment[0], anchor)

    moment = beta_one * first_moment[0] + (1.0 - beta_one) * gradient
    second = beta_two * second_moment[0] + (1.0 - beta_two) * gradient * gradient
    pseudo_grad = pseudo / replicas
    velocity = outer_mom * outer_velocity + pseudo_grad
    new_anchor = anchor - outer_rate * (pseudo_grad + outer_mom * velocity)
    return (moment[None], second[None], new_anchor, velocity)


def solution(mesh):
    return jax.shard_map(
        shards,
        mesh=mesh,
        in_specs=(
            P("replica", "fsdp", None),
            P("replica", "fsdp", None),
            P("replica", None, "fsdp"),
            P("replica", None, "fsdp"),
            P("replica", None, "fsdp"),
            P(None, "fsdp"),
            P(None, "fsdp"),
        ),
        out_specs=(
            P("replica", None, "fsdp"),
            P("replica", None, "fsdp"),
            P(None, "fsdp"),
            P(None, "fsdp"),
        ),
        check_vma=False,
    )
```

```python
import functools

import jax
import jax.numpy as jnp
from jax import lax
from jax.experimental import pallas as pl
from jax.experimental.pallas import tpu as pltpu
from jax.sharding import PartitionSpec as P

beta_one = 0.9
beta_two = 0.95
inner_rate = 0.1
decay_rate = 0.1
adam_eps = 1e-08
clip_eps = 1e-06
outer_rate = 0.7
outer_mom = 0.9
bias_one = 1.0 - 0.9**50
bias_two = 1.0 - 0.95**50

MESH = pl.DeviceIdType.MESH
LANES = 128
PAD = 16
REACH = 86.0
RING = 4
ITEMS = 8


def column_scale(values):
    largest = jnp.max(jnp.abs(values), axis=0, keepdims=True)
    return (largest * 1.01 + 1e-30).astype(jnp.bfloat16).astype(jnp.float32)


def encode(message, parts):
    rows = parts[0].shape[0]
    bounds = []
    for n, values in enumerate(parts):
        bound = column_scale(values)
        message[n * rows : (n + 1) * rows, :] = jnp.exp(values * (REACH / bound)).astype(jnp.bfloat16)
        bounds.append(bound)
    base = len(parts) * rows
    if len(parts) == 1:
        block = jnp.broadcast_to(bounds[0], (PAD, LANES))
    else:
        upper = lax.broadcasted_iota(jnp.int32, (PAD, LANES), 0) < PAD // 2
        block = jnp.where(upper, bounds[0], bounds[1])
    message[base : base + PAD, :] = block.astype(jnp.bfloat16)


def decode(message, count, which, rows):
    base = count * rows
    block = message[base : base + PAD, :].astype(jnp.float32)
    row = which * (PAD // 2) if count > 1 else 0
    bound = block[row : row + 1, :] * (1.0 / REACH)
    return jnp.log(message[which * rows : (which + 1) * rows, :].astype(jnp.float32)) * bound


def kernel(
    cotangent, act_t, inner, first, second, anchor, velocity,
    first_out, second_out, anchor_out, velocity_out,
    cot, inner_v, first_v, second_v, anchor_v, velocity_v,
    partial, send_a, recv_a, send_b, recv_b, send_z, recv_z,
    norm_send, norm_recv, half_send, half_recv, swap_send, swap_recv, pseudo,
    cot_sem, state_sem, sa_sem, ra_sem, sb_sem, rb_sem, sz_sem, rz_sem,
    ns_sem, nr_sem, hs_sem, hr_sem, ws_sem, wr_sem, ts_sem, tr_sem,
):
    hidden, tokens = act_t.shape
    rows = hidden // 2
    width = 2 * LANES
    me = lax.axis_index("fsdp")
    rep = lax.axis_index("replica")
    x = me % RING
    y = (me // RING) % RING
    z = me // (RING * RING)
    core = rep % 2
    zh = rep // 2

    def at(px, py, pz):
        return {"fsdp": pz * (RING * RING) + py * RING + px}

    def twin(pzh, pcore):
        return {"replica": pzh * 2 + pcore}

    def along(axis, step):
        if axis == 0:
            return at((x + step) % RING, y, z)
        return at(x, (y + step) % RING, z)

    here = (x, y)
    pair = at(x, y, 1 - z)
    mate = twin(zh, 1 - core)
    partners = (twin(zh + 1 - 2 * (zh % 2), core), twin(RING - 1 - zh, core))
    norm_groups = (
        [along(0, step) for step in (1, 2, 3)],
        [along(1, step) for step in (1, 2, 3)] + [at(x, (y + step) % RING, 1 - z) for step in range(RING)],
    )

    halves = cotangent.shape[1] // 2

    def load(k):
        zz = (1 - z) if k == 0 else z
        return pltpu.make_async_copy(
            cotangent.at[:, pl.ds(pl.multiple_of(zz * halves, halves), halves)], cot.at[k], cot_sem.at[k])

    load(0).start()
    load(1).start()
    states = []
    for n, (src, dst) in enumerate((
        (inner, inner_v), (first, first_v), (second, second_v), (anchor, anchor_v), (velocity, velocity_v),
    )):
        states.append(pltpu.make_async_copy(src, dst, state_sem.at[n]))
        states[n].start()

    barrier = pltpu.get_barrier_semaphore()
    everyone = norm_groups[0] + norm_groups[1] + [mate, *partners]
    for device in everyone:
        pl.semaphore_signal(barrier, inc=1, device_id=device, device_id_type=MESH)
    load(0).wait()
    pl.semaphore_wait(barrier, len(everyone))

    def copy_a(s, axis, i, way):
        return pltpu.make_async_remote_copy(
            src_ref=send_a.at[s, i, way], dst_ref=recv_a.at[s, i, way],
            send_sem=sa_sem.at[s, i, way], recv_sem=ra_sem.at[s, i, way],
            device_id=along(axis, 1 if way == 0 else 3), device_id_type=MESH)

    def copy_b(s, axis, i, way):
        return pltpu.make_async_remote_copy(
            src_ref=send_b.at[s, i, way], dst_ref=recv_b.at[s, i, way],
            send_sem=sb_sem.at[s, i, way], recv_sem=rb_sem.at[s, i, way],
            device_id=along(axis, 1 if way == 0 else 3), device_id_type=MESH)

    def copy_z(s):
        return pltpu.make_async_remote_copy(
            src_ref=send_z.at[s], dst_ref=recv_z.at[s], send_sem=sz_sem.at[s], recv_sem=rz_sem.at[s],
            device_id=pair, device_id_type=MESH)

    def offset(i):
        j = i % RING
        return jnp.where(j == 0, 2, jnp.where(j == 1, 1, jnp.where(j == 2, 3, 0)))

    def product(s, i, t):
        w = (here[1 - s] + offset(i)) % RING
        chunk = w * RING + t if s == 0 else t * RING + w
        columns = pl.ds(pl.multiple_of(chunk * width, width), width)
        return jnp.dot(act_t[s * rows : (s + 1) * rows, :], cot[i // RING, :, columns], preferred_element_type=jnp.float32)

    def round_a(s, axis, i, own):
        opposite = own(s, i, (here[axis] + 2) % RING)
        encode(send_a.at[s, i, 0], [opposite[:, :LANES]])
        copy_a(s, axis, i, 0).start()
        encode(send_a.at[s, i, 1], [opposite[:, LANES:]])
        copy_a(s, axis, i, 1).start()

    def round_b(s, axis, i, own):
        for way in range(2):
            value = own(s, i, (here[axis] + (1 if way == 0 else 3)) % RING)
            copy_a(s, axis, i, way).wait_recv()
            arrived = decode(recv_a.at[s, i, way], 1, 0, rows)
            left, right = value[:, :LANES], value[:, LANES:]
            if way == 0:
                left = left + arrived
            else:
                right = right + arrived
            encode(send_b.at[s, i, way], [left, right])
            copy_b(s, axis, i, way).start()

    def round_c(s, axis, i, own):
        value = own(s, i, here[axis])
        for way in range(2):
            copy_b(s, axis, i, way).wait_recv()
        parts = []
        for n in range(2):
            parts.append(value[:, n * LANES : (n + 1) * LANES]
                         + decode(recv_b.at[s, i, 0], 2, n, rows) + decode(recv_b.at[s, i, 1], 2, n, rows))
        for way in range(2):
            copy_a(s, axis, i, way).wait_send()
            copy_b(s, axis, i, way).wait_send()
        return parts

    def summed(s, i, t):
        return partial[s, i - ITEMS, t]

    @pl.loop(0, ITEMS + 2)
    def _(step):
        @pl.when(step == RING)
        def _():
            load(1).wait()

        @pl.when(step < ITEMS)
        def _():
            for s in range(2):
                round_a(s, s, step, product)

        @pl.when(jnp.logical_and(step >= 1, step < ITEMS + 1))
        def _():
            for s in range(2):
                round_b(s, s, step - 1, product)

        @pl.when(step >= 2)
        def _():
            i = step - 2
            for s in range(2):
                parts = round_c(s, s, i, product)
                w = (here[1 - s] + offset(i)) % RING
                for n in range(2):
                    partial[s, i // RING, w, :, n * LANES : (n + 1) * LANES] = parts[n]

        later = ITEMS + (step - 2) // RING

        @pl.when(jnp.logical_or(step == 2, step == RING + 2))
        def _():
            for s in range(2):
                round_a(s, 1 - s, later, summed)

        @pl.when(jnp.logical_or(step == 4, step == RING + 4))
        def _():
            for s in range(2):
                round_b(s, 1 - s, later, summed)

        @pl.when(step == RING + 2)
        def _():
            for s in range(2):
                encode(send_z.at[s], round_c(s, 1 - s, ITEMS, summed))
                copy_z(s).start()

    for state in states:
        state.wait()
    last = ITEMS + 1
    total = jnp.zeros((8, LANES), jnp.float32)
    for s in range(2):
        copy_z(s).wait_recv()
        parts = round_c(s, 1 - s, last, summed)
        for n in range(2):
            value = parts[n] + decode(recv_z.at[s], 2, n, rows)
            first_out[s * rows : (s + 1) * rows, n * LANES : (n + 1) * LANES] = value
            total = total + jnp.sum((value * value).reshape(rows // 8, 8, LANES), axis=0)

    slot = 0
    sent = []
    for phase, group in enumerate(norm_groups):
        norm_send[phase] = total
        copies = [
            pltpu.make_async_remote_copy(
                src_ref=norm_send.at[phase], dst_ref=norm_recv.at[slot + n],
                send_sem=ns_sem.at[slot + n], recv_sem=nr_sem.at[slot + n],
                device_id=device, device_id_type=MESH)
            for n, device in enumerate(group)
        ]
        for copy in copies:
            copy.start()
        for n, copy in enumerate(copies):
            copy.wait_recv()
            total = total + norm_recv[slot + n]
        slot += len(group)
        sent += copies

    mean_square = jnp.sum(total) / (hidden * cotangent.shape[1])
    clip_factor = jnp.minimum(1.0, lax.rsqrt(jnp.full((1, LANES), mean_square + clip_eps, jnp.float32)))

    def difference(part, columns):
        gradient = first_out[part, columns] * clip_factor
        moment = beta_one * first_v[part, columns] + (1.0 - beta_one) * gradient
        square = beta_two * second_v[part, columns] + (1.0 - beta_two) * gradient * gradient
        first_out[part, columns] = moment
        second_out[part, columns] = square
        params = inner_v[part, columns]
        stepped = params - inner_rate * (
            moment / bias_one / (jnp.sqrt(square / bias_two) + adam_eps) + decay_rate * params)
        return anchor_v[part, columns] - stepped

    given = pl.ds(pl.multiple_of((1 - core) * LANES, LANES), LANES)
    kept = pl.ds(pl.multiple_of(core * LANES, LANES), LANES)
    parts = [slice(0, rows), slice(rows, hidden)]

    def to_mate(n):
        return pltpu.make_async_remote_copy(
            src_ref=half_send.at[n], dst_ref=half_recv.at[n], send_sem=hs_sem.at[n], recv_sem=hr_sem.at[n],
            device_id=mate, device_id_type=MESH)

    def swap(n, turn):
        return pltpu.make_async_remote_copy(
            src_ref=swap_send.at[n, turn], dst_ref=swap_recv.at[n, turn],
            send_sem=ws_sem.at[n, turn], recv_sem=wr_sem.at[n, turn],
            device_id=partners[(n + turn) % 2], device_id_type=MESH)

    def share(n):
        block = pseudo.at[core, n]
        return pltpu.make_async_remote_copy(
            src_ref=block, dst_ref=block, send_sem=ts_sem.at[n], recv_sem=tr_sem.at[n],
            device_id=mate, device_id_type=MESH)

    for n in range(2):
        half_send[n] = difference(parts[n], given)
        to_mate(n).start()
    mine = [difference(parts[n], kept) for n in range(2)]
    for n in range(2):
        to_mate(n).wait_recv()
        encode(swap_send.at[n, 0], [mine[n] + half_recv[n]])
        swap(n, 0).start()
    for n in range(2):
        own = decode(swap_send.at[n, 0], 1, 0, rows)
        swap(n, 0).wait_recv()
        encode(swap_send.at[n, 1], [own + decode(swap_recv.at[n, 0], 1, 0, rows)])
        swap(n, 1).start()

    def finish(n, which, columns):
        pseudo_grad = pseudo[which, n] / (2 * RING)
        moved = outer_mom * velocity_v[parts[n], columns] + pseudo_grad
        velocity_out[parts[n], columns] = moved
        anchor_out[parts[n], columns] = anchor_v[parts[n], columns] - outer_rate * (pseudo_grad + outer_mom * moved)

    for n in range(2):
        own = decode(swap_send.at[n, 1], 1, 0, rows)
        swap(n, 1).wait_recv()
        pseudo[core, n] = own + decode(swap_recv.at[n, 1], 1, 0, rows)
        share(n).start()
    for n in range(2):
        finish(n, core, kept)
    for copy in sent + [copy_z(0), copy_z(1), to_mate(0), to_mate(1)]:
        copy.wait_send()
    for n in range(2):
        for turn in range(2):
            swap(n, turn).wait_send()
    for n in range(2):
        share(n).wait_recv()
        finish(n, 1 - core, given)
    for n in range(2):
        share(n).wait_send()


def shards(out_grad, hidden_act, inner_params, first_moment, second_moment, anchor, outer_velocity):
    cotangent, act_t = out_grad[0], hidden_act[0].T
    hidden, tokens = act_t.shape
    columns = anchor.shape[1]
    rows = hidden // 2
    bf16, f32 = jnp.bfloat16, jnp.float32
    vmem, dma = pltpu.VMEM, pltpu.SemaphoreType.DMA
    count = ITEMS + 2
    anywhere = pl.BlockSpec(memory_space=pltpu.HBM)
    local = pl.BlockSpec(memory_space=pltpu.VMEM)
    moment, second, new_anchor, new_velocity = pl.pallas_call(
        kernel,
        out_shape=(jax.ShapeDtypeStruct((hidden, columns), f32),) * 4,
        in_specs=[anywhere, local] + [anywhere] * 5,
        out_specs=(local,) * 4,
        scratch_shapes=[
            vmem((2, tokens, cotangent.shape[1] // 2), bf16),
            *[vmem((hidden, columns), f32)] * 5,
            vmem((2, 2, RING, rows, columns), f32),
            vmem((2, count, 2, rows + PAD, LANES), bf16),
            vmem((2, count, 2, rows + PAD, LANES), bf16),
            vmem((2, count, 2, 2 * rows + PAD, LANES), bf16),
            vmem((2, count, 2, 2 * rows + PAD, LANES), bf16),
            vmem((2, 2 * rows + PAD, LANES), bf16),
            vmem((2, 2 * rows + PAD, LANES), bf16),
            vmem((2, 8, LANES), f32),
            vmem((10, 8, LANES), f32),
            vmem((2, rows, LANES), f32),
            vmem((2, rows, LANES), f32),
            vmem((2, 2, rows + PAD, LANES), bf16),
            vmem((2, 2, rows + PAD, LANES), bf16),
            vmem((2, 2, rows, LANES), f32),
            dma((2,)), dma((5,)),
            dma((2, count, 2)), dma((2, count, 2)), dma((2, count, 2)), dma((2, count, 2)),
            dma((2,)), dma((2,)), dma((10,)), dma((10,)), dma((2,)), dma((2,)),
            dma((2, 2)), dma((2, 2)), dma((2,)), dma((2,)),
        ],
        compiler_params=pltpu.CompilerParams(
            collective_id=0, has_side_effects=True, vmem_limit_bytes=52 * 1024 * 1024),
        cost_estimate=pl.CostEstimate(
            flops=2 * tokens * hidden * cotangent.shape[1], bytes_accessed=12_000_000, transcendentals=8_000_000),
    )(cotangent, act_t, inner_params[0], first_moment[0], second_moment[0], anchor, outer_velocity)
    return (moment[None], second[None], new_anchor, new_velocity)


def solution(mesh):
    return jax.shard_map(
        shards,
        mesh=mesh,
        in_specs=(
            P("replica", "fsdp", None),
            P("replica", "fsdp", None),
            P("replica", None, "fsdp"),
            P("replica", None, "fsdp"),
            P("replica", None, "fsdp"),
            P(None, "fsdp"),
            P(None, "fsdp"),
        ),
        out_specs=(
            P("replica", None, "fsdp"),
            P("replica", None, "fsdp"),
            P(None, "fsdp"),
            P(None, "fsdp"),
        ),
        check_vma=False,
    )
```

```python
import functools

import jax
import jax.numpy as jnp
from jax import lax
from jax.experimental import pallas as pl
from jax.experimental.pallas import tpu as pltpu
from jax.sharding import PartitionSpec as P

beta_one = 0.9
beta_two = 0.95
inner_rate = 0.1
decay_rate = 0.1
adam_eps = 1e-08
clip_eps = 1e-06
outer_rate = 0.7
outer_mom = 0.9
bias_one = 1.0 - 0.9**50
bias_two = 1.0 - 0.95**50

MESH = pl.DeviceIdType.MESH
LANES = 128
PAD = 16
REACH = 86.0
RING = 4
ITEMS = 8
SPANS = ((0, 128), (128, 192), (320, 128))
COUNTS = (ITEMS + 2, ITEMS + 2, RING + 1)
ROUND_A, ROUND_B, ROUND_C, EARLY, CROSS = range(5)
SCHEDULE = (
    (0, 0, 0), (0, 1, 0), (3, 2, 2), (0, 0, 4), (0, 1, 1), (0, 0, 6), (0, 1, 6), (0, 0, 2),
    (0, 0, 1), (3, 2, 0), (0, 0, 3), (0, 0, 5), (3, 2, 1), (0, 1, 3), (1, 0, 0), (0, 1, 2),
    (3, 2, 4), (0, 1, 4), (1, 1, 0), (1, 0, 4), (3, 2, 6), (1, 0, 2), (1, 0, 6), (1, 1, 1),
    (3, 2, 3), (0, 2, 0), (0, 2, 1), (0, 0, 7), (1, 1, 2), (1, 1, 4), (0, 1, 5), (2, 1, 0),
    (0, 1, 8), (1, 0, 1), (2, 0, 4), (1, 2, 0), (1, 1, 3), (0, 2, 2), (2, 1, 1), (2, 0, 6),
    (1, 0, 5), (3, 2, 5), (1, 1, 6), (2, 0, 0), (2, 0, 2), (0, 0, 8), (2, 1, 2), (1, 1, 8),
    (1, 2, 1), (0, 1, 7), (2, 0, 1), (2, 2, 0), (0, 2, 3), (3, 2, 7), (1, 1, 5), (1, 2, 2),
    (2, 1, 4), (0, 2, 4), (0, 1, 9), (1, 0, 3), (0, 0, 9), (1, 0, 8), (2, 1, 3), (1, 1, 7),
    (1, 0, 7), (2, 1, 6), (1, 2, 3), (2, 2, 1), (2, 0, 5), (2, 2, 2), (4, 1, 8), (1, 2, 4),
    (1, 0, 9), (2, 1, 5), (1, 1, 9), (2, 0, 3), (4, 0, 8), (2, 2, 3), (2, 2, 4), (2, 1, 7),
    (2, 0, 7), (2, 0, 9), (2, 1, 9),
)


def column_scale(values):
    largest = jnp.max(jnp.abs(values), axis=0, keepdims=True)
    return (largest * 1.01 + 1e-30).astype(jnp.bfloat16).astype(jnp.float32)


def encode(message, parts):
    rows = parts[0].shape[0]
    bounds = []
    for n, values in enumerate(parts):
        bound = column_scale(values)
        message[n * rows : (n + 1) * rows, :] = jnp.exp(values * (REACH / bound)).astype(jnp.bfloat16)
        bounds.append(bound)
    base = len(parts) * rows
    share = PAD // len(parts)
    line = lax.broadcasted_iota(jnp.int32, (PAD, LANES), 0)
    block = jnp.broadcast_to(bounds[-1], (PAD, LANES))
    for n in range(len(parts) - 2, -1, -1):
        block = jnp.where(line < (n + 1) * share, bounds[n], block)
    message[base : base + PAD, :] = block.astype(jnp.bfloat16)


def decode(message, count, which, rows):
    base = count * rows
    block = message[base : base + PAD, :].astype(jnp.float32)
    row = which * (PAD // count)
    bound = block[row : row + 1, :] * (1.0 / REACH)
    return jnp.log(message[which * rows : (which + 1) * rows, :].astype(jnp.float32)) * bound


def kernel(
    cotangent, act_t, inner, first, second, anchor, velocity,
    first_out, second_out, anchor_out, velocity_out,
    cot, inner_v, first_v, second_v, anchor_v, velocity_v,
    partial, other_partial, third_partial,
    send_a0, send_a1, send_a2, recv_a0, recv_a1, recv_a2, send_b0, send_b1, send_b2, recv_b0, recv_b1, recv_b2,
    send_z0, send_z1, recv_z0, recv_z1, send_early, recv_early,
    norm_send, norm_recv, half_send, half_recv, swap_send, swap_recv, pseudo,
    cot_sem, state_sem, sa_sem, ra_sem, sb_sem, rb_sem, sz_sem, rz_sem, se_sem, re_sem,
    ns_sem, nr_sem, hs_sem, hr_sem, ws_sem, wr_sem, ts_sem, tr_sem,
):
    hidden, tokens = act_t.shape
    half = hidden // 2
    width = 2 * LANES
    sums = (partial, other_partial, third_partial)
    send_a, recv_a = (send_a0, send_a1, send_a2), (recv_a0, recv_a1, recv_a2)
    send_b, recv_b = (send_b0, send_b1, send_b2), (recv_b0, recv_b1, recv_b2)
    send_z, recv_z = (send_z0, send_z1), (recv_z0, recv_z1)
    me = lax.axis_index("fsdp")
    rep = lax.axis_index("replica")
    x = me % RING
    y = (me // RING) % RING
    z = me // (RING * RING)
    core = rep % 2
    zh = rep // 2

    def at(px, py, pz):
        return {"fsdp": pz * (RING * RING) + py * RING + px}

    def twin(pzh, pcore):
        return {"replica": pzh * 2 + pcore}

    def along(axis, step):
        if axis == 0:
            return at((x + step) % RING, y, z)
        return at(x, (y + step) % RING, z)

    here = (x, y)
    pair = at(x, y, 1 - z)
    mate = twin(zh, 1 - core)
    partners = (twin(zh + 1 - 2 * (zh % 2), core), twin(RING - 1 - zh, core))
    norm_groups = (
        [along(0, step) for step in (1, 2, 3)],
        [along(1, step) for step in (1, 2, 3)] + [at(x, (y + step) % RING, 1 - z) for step in range(RING)],
    )

    halves = cotangent.shape[1] // 2

    def load(k):
        zz = (1 - z) if k == 0 else z
        return pltpu.make_async_copy(
            cotangent.at[:, pl.ds(pl.multiple_of(zz * halves, halves), halves)], cot.at[k], cot_sem.at[k])

    load(0).start()
    load(1).start()
    states = []
    for n, (src, dst) in enumerate((
        (inner, inner_v), (first, first_v), (second, second_v), (anchor, anchor_v), (velocity, velocity_v),
    )):
        states.append(pltpu.make_async_copy(src, dst, state_sem.at[n]))
        states[n].start()

    barrier = pltpu.get_barrier_semaphore()
    everyone = norm_groups[0] + norm_groups[1] + [mate, *partners]
    for device in everyone:
        pl.semaphore_signal(barrier, inc=1, device_id=device, device_id_type=MESH)
    def copy_a(s, axis, i, way):
        return pltpu.make_async_remote_copy(
            src_ref=send_a[s].at[i, way], dst_ref=recv_a[s].at[i, way],
            send_sem=sa_sem.at[s, i, way], recv_sem=ra_sem.at[s, i, way],
            device_id=along(axis, 1 if way == 0 else 3), device_id_type=MESH)

    def copy_b(s, axis, i, way):
        return pltpu.make_async_remote_copy(
            src_ref=send_b[s].at[i, way], dst_ref=recv_b[s].at[i, way],
            send_sem=sb_sem.at[s, i, way], recv_sem=rb_sem.at[s, i, way],
            device_id=along(axis, 1 if way == 0 else 3), device_id_type=MESH)

    def copy_z(s):
        return pltpu.make_async_remote_copy(
            src_ref=send_z[s], dst_ref=recv_z[s], send_sem=sz_sem.at[s], recv_sem=rz_sem.at[s],
            device_id=pair, device_id_type=MESH)

    def copy_early(j):
        return pltpu.make_async_remote_copy(
            src_ref=send_early.at[j], dst_ref=recv_early.at[j], send_sem=se_sem.at[j], recv_sem=re_sem.at[j],
            device_id=pair, device_id_type=MESH)

    def offset(i):
        return (2, 1, 3, 0)[i % RING]

    def dot(s, k, chunk):
        columns = pl.ds(pl.multiple_of(chunk * width, width), width)
        first_row, rows = SPANS[s]
        return jnp.dot(act_t[first_row : first_row + rows, :], cot[k, :, columns], preferred_element_type=jnp.float32)

    def product(s, i, step):
        w = (here[1 - s] + offset(i)) % RING
        t = (here[s] + step) % RING
        return dot(s, i // RING, w * RING + t if s == 0 else t * RING + w)

    def paired(s, n, step):
        order = (2, 1, 3, 0).index(step)
        w = (y + offset(n)) % RING
        t = (x + step) % RING
        j = 2 * n + order // 2
        if order in (0, 2):
            copy_early(j).wait_recv()
        _, rows = SPANS[s]
        arrived = recv_early.at[j]
        both = [decode(arrived, 4, 2 * (order % 2) + h, rows) for h in range(2)]
        return dot(s, 1, w * RING + t) + jnp.concatenate(both, axis=1)

    def summed(s, i, step):
        axis = 1 if s != 1 else 0
        k = i - ITEMS if s < 2 else 0
        return sums[s][k, (here[axis] + step) % RING]

    def fill_a(s, axis, i, own):
        opposite = own(s, i, 2)
        encode(send_a[s].at[i, 0], [opposite[:, :LANES]])
        encode(send_a[s].at[i, 1], [opposite[:, LANES:]])

    def start_a(s, axis, i):
        for way in range(2):
            copy_a(s, axis, i, way).start()

    def round_a(s, axis, i, own):
        fill_a(s, axis, i, own)
        start_a(s, axis, i)

    def round_b(s, axis, i, own):
        _, rows = SPANS[s]
        for way in range(2):
            value = own(s, i, 1 if way == 0 else 3)
            copy_a(s, axis, i, way).wait_recv()
            arrived = decode(recv_a[s].at[i, way], 1, 0, rows)
            left, right = value[:, :LANES], value[:, LANES:]
            if way == 0:
                left = left + arrived
            else:
                right = right + arrived
            encode(send_b[s].at[i, way], [left, right])
            copy_b(s, axis, i, way).start()

    def round_c(s, axis, i, own):
        _, rows = SPANS[s]
        value = own(s, i, 0)
        for way in range(2):
            copy_b(s, axis, i, way).wait_recv()
        parts = []
        for n in range(2):
            parts.append(value[:, n * LANES : (n + 1) * LANES]
                         + decode(recv_b[s].at[i, 0], 2, n, rows) + decode(recv_b[s].at[i, 1], 2, n, rows))
        for way in range(2):
            copy_a(s, axis, i, way).wait_send()
            copy_b(s, axis, i, way).wait_send()
        return parts

    def keep(s, k, w, parts):
        for n in range(2):
            sums[s][k, w, :, n * LANES : (n + 1) * LANES] = parts[n]

    def send_pair(j):
        w = (y + offset(j // 2)) % RING
        parts = []
        for step in ((2, 1), (3, 0))[j % 2]:
            value = dot(2, 0, w * RING + (x + step) % RING)
            parts += [value[:, :LANES], value[:, LANES:]]
        encode(send_early.at[j], parts)
        copy_early(j).start()

    total = jnp.zeros((8, LANES), jnp.float32)
    loaded = False
    load(0).wait()
    for s in range(2):
        fill_a(s, s, 0, product)
    pl.semaphore_wait(barrier, len(everyone))
    for s in range(2):
        start_a(s, s, 0)
    for task, s, i in SCHEDULE[2:]:
        later = i >= COUNTS[s] - (2 if s < 2 else 1)
        axis = (1 if s == 0 else 0) if later and s < 2 else (1 if later or s == 1 else 0)
        own = summed if later else (product if s < 2 else paired)
        if not loaded and not later and task in (ROUND_A, ROUND_B, ROUND_C) and (s == 2 or i >= RING):
            load(1).wait()
            loaded = True
        if task == EARLY:
            send_pair(i)
        elif task == CROSS:
            encode(send_z[s], round_c(s, 1 - s, ITEMS, summed))
            copy_z(s).start()
        elif task == ROUND_A:
            round_a(s, axis, i, own)
        elif task == ROUND_B:
            round_b(s, axis, i, own)
        elif not later:
            keep(s, i // RING, ((here[1 - s] if s < 2 else y) + offset(i)) % RING, round_c(s, axis, i, own))
        elif i == COUNTS[s] - 1:
            first_row, rows = SPANS[s]
            parts = round_c(s, axis, i, own)
            if s < 2:
                copy_z(s).wait_recv()
            for n in range(2):
                value = parts[n]
                if s < 2:
                    value = value + decode(recv_z[s], 2, n, rows)
                first_out[first_row : first_row + rows, n * LANES : (n + 1) * LANES] = value
                total = total + jnp.sum((value * value).reshape(rows // 8, 8, LANES), axis=0)
    for state in states:
        state.wait()

    slot = 0
    sent = []
    for phase, group in enumerate(norm_groups):
        norm_send[phase] = total
        copies = [
            pltpu.make_async_remote_copy(
                src_ref=norm_send.at[phase], dst_ref=norm_recv.at[slot + n],
                send_sem=ns_sem.at[slot + n], recv_sem=nr_sem.at[slot + n],
                device_id=device, device_id_type=MESH)
            for n, device in enumerate(group)
        ]
        for copy in copies:
            copy.start()
        for n, copy in enumerate(copies):
            copy.wait_recv()
            total = total + norm_recv[slot + n]
        slot += len(group)
        sent += copies

    mean_square = jnp.sum(total) / (hidden * cotangent.shape[1])
    clip_factor = jnp.minimum(1.0, lax.rsqrt(jnp.full((1, LANES), mean_square + clip_eps, jnp.float32)))

    def difference(part, columns):
        gradient = first_out[part, columns] * clip_factor
        moment = beta_one * first_v[part, columns] + (1.0 - beta_one) * gradient
        square = beta_two * second_v[part, columns] + (1.0 - beta_two) * gradient * gradient
        first_out[part, columns] = moment
        second_out[part, columns] = square
        params = inner_v[part, columns]
        stepped = params - inner_rate * (
            moment / bias_one / (jnp.sqrt(square / bias_two) + adam_eps) + decay_rate * params)
        return anchor_v[part, columns] - stepped

    given = pl.ds(pl.multiple_of((1 - core) * LANES, LANES), LANES)
    kept = pl.ds(pl.multiple_of(core * LANES, LANES), LANES)
    parts = [slice(0, half), slice(half, hidden)]

    def to_mate(n):
        return pltpu.make_async_remote_copy(
            src_ref=half_send.at[n], dst_ref=half_recv.at[n], send_sem=hs_sem.at[n], recv_sem=hr_sem.at[n],
            device_id=mate, device_id_type=MESH)

    def swap(n, turn):
        return pltpu.make_async_remote_copy(
            src_ref=swap_send.at[n, turn], dst_ref=swap_recv.at[n, turn],
            send_sem=ws_sem.at[n, turn], recv_sem=wr_sem.at[n, turn],
            device_id=partners[(n + turn) % 2], device_id_type=MESH)

    def share(n):
        block = pseudo.at[core, n]
        return pltpu.make_async_remote_copy(
            src_ref=block, dst_ref=block, send_sem=ts_sem.at[n], recv_sem=tr_sem.at[n],
            device_id=mate, device_id_type=MESH)

    for n in range(2):
        half_send[n] = difference(parts[n], given)
        to_mate(n).start()
    mine = [difference(parts[n], kept) for n in range(2)]
    for n in range(2):
        to_mate(n).wait_recv()
        encode(swap_send.at[n, 0], [mine[n] + half_recv[n]])
        swap(n, 0).start()
    for n in range(2):
        own = decode(swap_send.at[n, 0], 1, 0, half)
        swap(n, 0).wait_recv()
        encode(swap_send.at[n, 1], [own + decode(swap_recv.at[n, 0], 1, 0, half)])
        swap(n, 1).start()

    def finish(n, which, columns):
        pseudo_grad = pseudo[which, n] / (2 * RING)
        moved = outer_mom * velocity_v[parts[n], columns] + pseudo_grad
        velocity_out[parts[n], columns] = moved
        anchor_out[parts[n], columns] = anchor_v[parts[n], columns] - outer_rate * (pseudo_grad + outer_mom * moved)

    for n in range(2):
        own = decode(swap_send.at[n, 1], 1, 0, half)
        swap(n, 1).wait_recv()
        pseudo[core, n] = own + decode(swap_recv.at[n, 1], 1, 0, half)
        share(n).start()
    for n in range(2):
        finish(n, core, kept)
    for copy in sent + [copy_z(0), copy_z(1), to_mate(0), to_mate(1)] + [copy_early(j) for j in range(ITEMS)]:
        copy.wait_send()
    for n in range(2):
        for turn in range(2):
            swap(n, turn).wait_send()
    for n in range(2):
        share(n).wait_recv()
        finish(n, 1 - core, given)
    for n in range(2):
        share(n).wait_send()


def place(*refs):
    count = len(refs) // 2
    sems = refs[-1]
    copies = [pltpu.make_async_copy(refs[n], refs[count + n], sems.at[n]) for n in range(count)]
    for copy in copies:
        copy.start()
    for copy in copies:
        copy.wait()


def shards(out_grad, hidden_act, inner_params, first_moment, second_moment, anchor, outer_velocity):
    cotangent, act_t = out_grad[0], hidden_act[0].T
    hidden, tokens = act_t.shape
    columns = anchor.shape[1]
    half = hidden // 2
    bf16, f32 = jnp.bfloat16, jnp.float32
    vmem, dma = pltpu.VMEM, pltpu.SemaphoreType.DMA
    count = ITEMS + 2
    anywhere = pl.BlockSpec(memory_space=pltpu.HBM)
    local = pl.BlockSpec(memory_space=pltpu.VMEM)
    moment, second, new_anchor, new_velocity = pl.pallas_call(
        kernel,
        out_shape=(jax.ShapeDtypeStruct((hidden, columns), f32),) * 4,
        in_specs=[anywhere, local] + [anywhere] * 5,
        out_specs=(local,) * 4,
        scratch_shapes=[
            vmem((2, tokens, cotangent.shape[1] // 2), bf16),
            *[vmem((hidden, columns), f32)] * 5,
            *[vmem((2 if s < 2 else 1, RING, rows, columns), f32) for s, (_, rows) in enumerate(SPANS)],
            *[vmem((count, 2, rows + PAD, LANES), bf16) for count, (_, rows) in zip(COUNTS, SPANS)] * 2,
            *[vmem((count, 2, 2 * rows + PAD, LANES), bf16) for count, (_, rows) in zip(COUNTS, SPANS)] * 2,
            *[vmem((2 * rows + PAD, LANES), bf16) for _, rows in SPANS[:2]] * 2,
            *[vmem((ITEMS, 4 * SPANS[2][1] + PAD, LANES), bf16)] * 2,
            vmem((2, 8, LANES), f32),
            vmem((10, 8, LANES), f32),
            vmem((2, half, LANES), f32),
            vmem((2, half, LANES), f32),
            vmem((2, 2, half + PAD, LANES), bf16),
            vmem((2, 2, half + PAD, LANES), bf16),
            vmem((2, 2, half, LANES), f32),
            dma((2,)), dma((5,)),
            *[dma((3, count, 2))] * 4,
            dma((2,)), dma((2,)), dma((ITEMS,)), dma((ITEMS,)), dma((10,)), dma((10,)), dma((2,)), dma((2,)),
            dma((2, 2)), dma((2, 2)), dma((2,)), dma((2,)),
        ],
        compiler_params=pltpu.CompilerParams(
            collective_id=0, has_side_effects=True, vmem_limit_bytes=52 * 1024 * 1024),
        cost_estimate=pl.CostEstimate(
            flops=2 * tokens * hidden * cotangent.shape[1], bytes_accessed=12_000_000, transcendentals=8_000_000),
    )(cotangent, act_t, inner_params[0], first_moment[0], second_moment[0], anchor, outer_velocity)
    moment, second, new_anchor, new_velocity = pl.pallas_call(
        place,
        out_shape=(jax.ShapeDtypeStruct((hidden, columns), f32),) * 4,
        in_specs=[local] * 4,
        out_specs=(anywhere,) * 4,
        scratch_shapes=[dma((4,))],
        compiler_params=pltpu.CompilerParams(vmem_limit_bytes=4 * 1024 * 1024),
        cost_estimate=pl.CostEstimate(flops=0, bytes_accessed=32 * hidden * columns, transcendentals=0),
    )(moment, second, new_anchor, new_velocity)
    return (moment[None], second[None], new_anchor, new_velocity)


def solution(mesh):
    return jax.shard_map(
        shards,
        mesh=mesh,
        in_specs=(
            P("replica", "fsdp", None),
            P("replica", "fsdp", None),
            P("replica", None, "fsdp"),
            P("replica", None, "fsdp"),
            P("replica", None, "fsdp"),
            P(None, "fsdp"),
            P(None, "fsdp"),
        ),
        out_specs=(
            P("replica", None, "fsdp"),
            P("replica", None, "fsdp"),
            P(None, "fsdp"),
            P(None, "fsdp"),
        ),
        check_vma=False,
    )
```

```python
import functools

import jax
import jax.numpy as jnp
from jax import lax
from jax.experimental import pallas as pl
from jax.experimental.pallas import tpu as pltpu
from jax.sharding import PartitionSpec as P

beta_one = 0.9
beta_two = 0.95
inner_rate = 0.1
decay_rate = 0.1
adam_eps = 1e-08
clip_eps = 1e-06
outer_rate = 0.7
outer_mom = 0.9
bias_one = 1.0 - 0.9**50
bias_two = 1.0 - 0.95**50

MESH = pl.DeviceIdType.MESH
LANES = 128
PAD = 16
REACH = 86.0
RING = 4
ITEMS = 8
BLOCKS = (128, 192, 144)
COUNTS = (ITEMS + 2, ITEMS + 2, RING + 1)
ROUND_A, ROUND_B, ROUND_C, EARLY, CROSS = range(5)
SCHEDULE = (
    (0, 0, 0), (0, 1, 0), (3, 2, 0), (0, 0, 7), (0, 0, 2), (3, 2, 4), (0, 1, 4), (0, 0, 1),
    (0, 1, 2), (0, 1, 1), (0, 0, 3), (0, 0, 4), (1, 0, 0), (0, 1, 6), (3, 2, 2), (0, 0, 5),
    (1, 1, 0), (1, 0, 2), (0, 0, 6), (1, 0, 3), (0, 2, 0), (1, 1, 1), (1, 1, 2), (3, 2, 1),
    (0, 1, 3), (1, 0, 4), (2, 0, 0), (2, 1, 0), (3, 2, 6), (0, 1, 8), (0, 2, 2), (0, 1, 5),
    (3, 2, 5), (2, 0, 2), (1, 0, 5), (0, 0, 8), (1, 1, 4), (1, 0, 1), (3, 2, 3), (2, 0, 4),
    (1, 0, 6), (2, 1, 1), (1, 1, 6), (2, 1, 2), (2, 0, 3), (1, 2, 0), (1, 1, 3), (0, 0, 9),
    (0, 2, 1), (3, 2, 7), (1, 1, 8), (0, 2, 3), (2, 0, 1), (1, 0, 8), (2, 1, 4), (0, 1, 7),
    (2, 0, 6), (1, 1, 5), (2, 0, 5), (2, 2, 0), (0, 1, 9), (1, 2, 2), (2, 1, 3), (0, 2, 4),
    (1, 0, 9), (1, 2, 1), (1, 0, 7), (1, 1, 7), (1, 2, 3), (4, 1, 8), (2, 2, 2), (2, 1, 6),
    (2, 1, 5), (1, 1, 9), (2, 2, 1), (1, 2, 4), (4, 0, 8), (2, 0, 7), (2, 0, 9), (2, 2, 3),
    (2, 1, 7), (2, 2, 4), (2, 1, 9),
)


def column_scale(values):
    largest = jnp.max(jnp.abs(values), axis=0, keepdims=True)
    return (largest * 1.01 + 1e-30).astype(jnp.bfloat16).astype(jnp.float32)


def last_line():
    return lax.broadcasted_iota(jnp.int32, (PAD, LANES), 0) == PAD - 1


def encode(message, parts):
    rows = parts[0].shape[0]
    for n, values in enumerate(parts):
        bound = column_scale(values)
        coded = jnp.exp(values * (REACH / bound))
        end = (n + 1) * rows
        message[n * rows : end - PAD, :] = coded[: rows - PAD].astype(jnp.bfloat16)
        message[end - PAD : end, :] = jnp.where(last_line(), bound, coded[rows - PAD :]).astype(jnp.bfloat16)


def decode(message, which, rows):
    block = message[which * rows : (which + 1) * rows, :].astype(jnp.float32)
    values = jnp.log(block) * (block[rows - 1 : rows, :] * (1.0 / REACH))
    return jnp.concatenate([values[: rows - PAD], jnp.where(last_line(), 0.0, values[rows - PAD :])], axis=0)


def kernel(
    cotangent, activations, inner, first, second, anchor, velocity,
    first_out, second_out, anchor_out, velocity_out,
    cot, act_t, inner_v, first_v, second_v, anchor_v, velocity_v,
    partial, other_partial, third_partial,
    send_a0, send_a1, send_a2, recv_a0, recv_a1, recv_a2, send_b0, send_b1, send_b2, recv_b0, recv_b1, recv_b2,
    send_z0, send_z1, recv_z0, recv_z1, send_early, recv_early,
    norm_send, norm_recv, half_send, half_recv, swap_send, swap_recv, pseudo,
    cot_sem, state_sem, sa_sem, ra_sem, sb_sem, rb_sem, sz_sem, rz_sem, se_sem, re_sem,
    ns_sem, nr_sem, hs_sem, hr_sem, ws_sem, wr_sem, ts_sem, tr_sem,
):
    hidden, tokens = activations.shape
    piece = hidden // RING
    width = 2 * LANES
    sums = (partial, other_partial, third_partial)
    send_a, recv_a = (send_a0, send_a1, send_a2), (recv_a0, recv_a1, recv_a2)
    send_b, recv_b = (send_b0, send_b1, send_b2), (recv_b0, recv_b1, recv_b2)
    send_z, recv_z = (send_z0, send_z1), (recv_z0, recv_z1)
    me = lax.axis_index("fsdp")
    rep = lax.axis_index("replica")
    x = me % RING
    y = (me // RING) % RING
    z = me // (RING * RING)
    core = rep % 2
    zh = rep // 2

    def at(px, py, pz):
        return {"fsdp": pz * (RING * RING) + py * RING + px}

    def twin(pzh, pcore):
        return {"replica": pzh * 2 + pcore}

    def along(axis, step):
        if axis == 0:
            return at((x + step) % RING, y, z)
        return at(x, (y + step) % RING, z)

    here = (x, y)
    pair = at(x, y, 1 - z)
    mate = twin(zh, 1 - core)
    partners = (twin(zh + 1 - 2 * (zh % 2), core), twin(RING - 1 - zh, core))
    norm_groups = (
        [along(0, step) for step in (1, 2, 3)],
        [along(1, step) for step in (1, 2, 3)] + [at(x, (y + step) % RING, 1 - z) for step in range(RING)],
    )

    halves = cotangent.shape[1] // 2

    def load(k):
        zz = (1 - z) if k == 0 else z
        return pltpu.make_async_copy(
            cotangent.at[:, pl.ds(pl.multiple_of(zz * halves, halves), halves)], cot.at[k], cot_sem.at[k])

    load(0).start()
    load(1).start()
    states = []
    for n, (src, dst) in enumerate((
        (inner, inner_v), (first, first_v), (second, second_v), (anchor, anchor_v), (velocity, velocity_v),
    )):
        states.append(pltpu.make_async_copy(src, dst, state_sem.at[n]))
        states[n].start()

    barrier = pltpu.get_barrier_semaphore()
    everyone = norm_groups[0] + norm_groups[1] + [mate, *partners]
    for device in everyone:
        pl.semaphore_signal(barrier, inc=1, device_id=device, device_id_type=MESH)
    def copy_a(s, axis, i, way):
        return pltpu.make_async_remote_copy(
            src_ref=send_a[s].at[i, way], dst_ref=recv_a[s].at[i, way],
            send_sem=sa_sem.at[s, i, way], recv_sem=ra_sem.at[s, i, way],
            device_id=along(axis, 1 if way == 0 else 3), device_id_type=MESH)

    def copy_b(s, axis, i, way):
        return pltpu.make_async_remote_copy(
            src_ref=send_b[s].at[i, way], dst_ref=recv_b[s].at[i, way],
            send_sem=sb_sem.at[s, i, way], recv_sem=rb_sem.at[s, i, way],
            device_id=along(axis, 1 if way == 0 else 3), device_id_type=MESH)

    def copy_z(s):
        return pltpu.make_async_remote_copy(
            src_ref=send_z[s], dst_ref=recv_z[s], send_sem=sz_sem.at[s], recv_sem=rz_sem.at[s],
            device_id=pair, device_id_type=MESH)

    def copy_early(j):
        return pltpu.make_async_remote_copy(
            src_ref=send_early.at[j], dst_ref=recv_early.at[j], send_sem=se_sem.at[j], recv_sem=re_sem.at[j],
            device_id=pair, device_id_type=MESH)

    def offset(i):
        return (2, 1, 3, 0)[i % RING]

    def dot(s, k, chunk):
        columns = pl.ds(pl.multiple_of(chunk * width, width), width)
        first_row, rows = sum(BLOCKS[:s]), BLOCKS[s]
        return jnp.dot(act_t[first_row : first_row + rows, :], cot[k, :, columns], preferred_element_type=jnp.float32)

    def product(s, i, step):
        w = (here[1 - s] + offset(i)) % RING
        t = (here[s] + step) % RING
        return dot(s, i // RING, w * RING + t if s == 0 else t * RING + w)

    def paired(s, n, step):
        order = (2, 1, 3, 0).index(step)
        w = (y + offset(n)) % RING
        t = (x + step) % RING
        j = 2 * n + order // 2
        if order in (0, 2):
            copy_early(j).wait_recv()
        rows = BLOCKS[s]
        arrived = recv_early.at[j]
        both = [decode(arrived, 2 * (order % 2) + h, rows) for h in range(2)]
        return dot(s, 1, w * RING + t) + jnp.concatenate(both, axis=1)

    def summed(s, i, step):
        axis = 1 if s != 1 else 0
        k = i - ITEMS if s < 2 else 0
        return sums[s][k, (here[axis] + step) % RING]

    def fill_a(s, axis, i, own):
        opposite = own(s, i, 2)
        encode(send_a[s].at[i, 0], [opposite[:, :LANES]])
        encode(send_a[s].at[i, 1], [opposite[:, LANES:]])

    def start_a(s, axis, i):
        for way in range(2):
            copy_a(s, axis, i, way).start()

    def round_a(s, axis, i, own):
        fill_a(s, axis, i, own)
        start_a(s, axis, i)

    def round_b(s, axis, i, own):
        rows = BLOCKS[s]
        for way in range(2):
            value = own(s, i, 1 if way == 0 else 3)
            copy_a(s, axis, i, way).wait_recv()
            arrived = decode(recv_a[s].at[i, way], 0, rows)
            left, right = value[:, :LANES], value[:, LANES:]
            if way == 0:
                left = left + arrived
            else:
                right = right + arrived
            encode(send_b[s].at[i, way], [left, right])
            copy_b(s, axis, i, way).start()

    def round_c(s, axis, i, own):
        rows = BLOCKS[s]
        value = own(s, i, 0)
        for way in range(2):
            copy_b(s, axis, i, way).wait_recv()
        parts = []
        for n in range(2):
            parts.append(value[:, n * LANES : (n + 1) * LANES]
                         + decode(recv_b[s].at[i, 0], n, rows) + decode(recv_b[s].at[i, 1], n, rows))
        for way in range(2):
            copy_a(s, axis, i, way).wait_send()
            copy_b(s, axis, i, way).wait_send()
        return parts

    def keep(s, k, w, parts):
        for n in range(2):
            sums[s][k, w, :, n * LANES : (n + 1) * LANES] = parts[n]

    def send_pair(j):
        w = (y + offset(j // 2)) % RING
        parts = []
        for step in ((2, 1), (3, 0))[j % 2]:
            value = dot(2, 0, w * RING + (x + step) % RING)
            parts += [value[:, :LANES], value[:, LANES:]]
        encode(send_early.at[j], parts)
        copy_early(j).start()

    total = jnp.zeros((8, LANES), jnp.float32)
    loaded = False
    spares = []
    ends = (BLOCKS[0], hidden)
    inside = hidden - BLOCKS[0] - BLOCKS[2]
    middle = BLOCKS[0] + inside
    after = BLOCKS[0] + BLOCKS[1]
    line = lax.broadcasted_iota(jnp.int32, (PAD, tokens), 0)
    spare = jnp.zeros((PAD, tokens), jnp.float32)
    for n, (end, place_end) in enumerate(zip(ends, (BLOCKS[0], sum(BLOCKS)))):
        tail_rows = activations[end - PAD : end, :].astype(jnp.float32)
        act_t[place_end - PAD : place_end, :] = jnp.where(line == PAD - 1, 0.0, tail_rows).astype(jnp.bfloat16)
        spare = jnp.where(line == n, tail_rows[PAD - 1 : PAD, :], spare)
    act_t[: BLOCKS[0] - PAD, :] = activations[: BLOCKS[0] - PAD, :]
    act_t[BLOCKS[0] : middle, :] = activations[BLOCKS[0] : middle, :]
    act_t[middle : middle + PAD, :] = spare.astype(jnp.bfloat16)
    act_t[after : sum(BLOCKS) - PAD, :] = activations[middle : hidden - PAD, :]

    load(0).wait()
    for s in range(2):
        fill_a(s, s, 0, product)
    pl.semaphore_wait(barrier, len(everyone))
    for s in range(2):
        start_a(s, s, 0)
    for task, s, i in SCHEDULE[2:]:
        later = i >= COUNTS[s] - (2 if s < 2 else 1)
        axis = (1 if s == 0 else 0) if later and s < 2 else (1 if later or s == 1 else 0)
        own = summed if later else (product if s < 2 else paired)
        if not loaded and not later and task in (ROUND_A, ROUND_B, ROUND_C) and (s == 2 or i >= RING):
            load(1).wait()
            loaded = True
        if task == EARLY:
            send_pair(i)
        elif task == CROSS:
            encode(send_z[s], round_c(s, 1 - s, ITEMS, summed))
            copy_z(s).start()
        elif task == ROUND_A:
            round_a(s, axis, i, own)
        elif task == ROUND_B:
            round_b(s, axis, i, own)
        elif not later:
            keep(s, i // RING, ((here[1 - s] if s < 2 else y) + offset(i)) % RING, round_c(s, axis, i, own))
        elif i == COUNTS[s] - 1:
            rows = BLOCKS[s]
            start, taken = ((0, rows), (BLOCKS[0], inside), (middle, rows))[s]
            parts = round_c(s, axis, i, own)
            if s < 2:
                copy_z(s).wait_recv()
            for n in range(2):
                value = parts[n]
                if s < 2:
                    value = value + decode(recv_z[s], n, rows)
                first_out[start : start + taken, n * LANES : (n + 1) * LANES] = value[:taken]
                if s == 1:
                    spares.append(value[taken : taken + 8])
                total = total + jnp.sum((value * value).reshape(rows // 8, 8, LANES), axis=0)
    for n in range(2):
        for row, end in enumerate(ends):
            first_out[end - 1 : end, n * LANES : (n + 1) * LANES] = spares[n][row : row + 1]
    for state in states:
        state.wait()

    slot = 0
    sent = []
    for phase, group in enumerate(norm_groups):
        norm_send[phase] = total
        copies = [
            pltpu.make_async_remote_copy(
                src_ref=norm_send.at[phase], dst_ref=norm_recv.at[slot + n],
                send_sem=ns_sem.at[slot + n], recv_sem=nr_sem.at[slot + n],
                device_id=device, device_id_type=MESH)
            for n, device in enumerate(group)
        ]
        for copy in copies:
            copy.start()
        for n, copy in enumerate(copies):
            copy.wait_recv()
            total = total + norm_recv[slot + n]
        slot += len(group)
        sent += copies

    mean_square = jnp.sum(total) / (hidden * cotangent.shape[1])
    clip_factor = jnp.minimum(1.0, lax.rsqrt(jnp.full((1, LANES), mean_square + clip_eps, jnp.float32)))

    def difference(part, columns):
        gradient = first_out[part, columns] * clip_factor
        moment = beta_one * first_v[part, columns] + (1.0 - beta_one) * gradient
        square = beta_two * second_v[part, columns] + (1.0 - beta_two) * gradient * gradient
        first_out[part, columns] = moment
        second_out[part, columns] = square
        params = inner_v[part, columns]
        stepped = params - inner_rate * (
            moment / bias_one / (jnp.sqrt(square / bias_two) + adam_eps) + decay_rate * params)
        return anchor_v[part, columns] - stepped

    given = pl.ds(pl.multiple_of((1 - core) * LANES, LANES), LANES)
    kept = pl.ds(pl.multiple_of(core * LANES, LANES), LANES)
    parts = [slice(n * piece, (n + 1) * piece) for n in range(RING)]

    def to_mate(n):
        return pltpu.make_async_remote_copy(
            src_ref=half_send.at[n], dst_ref=half_recv.at[n], send_sem=hs_sem.at[n], recv_sem=hr_sem.at[n],
            device_id=mate, device_id_type=MESH)

    def swap(n, turn):
        return pltpu.make_async_remote_copy(
            src_ref=swap_send.at[n, turn], dst_ref=swap_recv.at[n, turn],
            send_sem=ws_sem.at[n, turn], recv_sem=wr_sem.at[n, turn],
            device_id=partners[(n + turn) % 2], device_id_type=MESH)

    def share(n):
        block = pseudo.at[core, n]
        return pltpu.make_async_remote_copy(
            src_ref=block, dst_ref=block, send_sem=ts_sem.at[n], recv_sem=tr_sem.at[n],
            device_id=mate, device_id_type=MESH)

    def widen(values):
        return jnp.concatenate([values, jnp.zeros((PAD, LANES), jnp.float32)], axis=0)

    for n in range(RING):
        half_send[n] = difference(parts[n], given)
        to_mate(n).start()
    mine = [difference(parts[n], kept) for n in range(RING)]
    for n in range(RING):
        to_mate(n).wait_recv()
        encode(swap_send.at[n, 0], [widen(mine[n] + half_recv[n])])
        swap(n, 0).start()
    for n in range(RING):
        own = decode(swap_send.at[n, 0], 0, piece + PAD)
        swap(n, 0).wait_recv()
        encode(swap_send.at[n, 1], [own + decode(swap_recv.at[n, 0], 0, piece + PAD)])
        swap(n, 1).start()

    def finish(n, which, columns):
        pseudo_grad = pseudo[which, n] / (2 * RING)
        moved = outer_mom * velocity_v[parts[n], columns] + pseudo_grad
        velocity_out[parts[n], columns] = moved
        anchor_out[parts[n], columns] = anchor_v[parts[n], columns] - outer_rate * (pseudo_grad + outer_mom * moved)

    for n in range(RING):
        own = decode(swap_send.at[n, 1], 0, piece + PAD)
        swap(n, 1).wait_recv()
        pseudo[core, n] = (own + decode(swap_recv.at[n, 1], 0, piece + PAD))[:piece]
        share(n).start()
    for n in range(RING):
        finish(n, core, kept)
    for copy in sent + [copy_z(0), copy_z(1), *[to_mate(n) for n in range(RING)]] + [copy_early(j) for j in range(ITEMS)]:
        copy.wait_send()
    for n in range(RING):
        for turn in range(2):
            swap(n, turn).wait_send()
    for n in range(RING):
        share(n).wait_recv()
        finish(n, 1 - core, given)
    for n in range(RING):
        share(n).wait_send()


def place(*refs):
    count = len(refs) // 2
    sems = refs[-1]
    copies = [pltpu.make_async_copy(refs[n], refs[count + n], sems.at[n]) for n in range(count)]
    for copy in copies:
        copy.start()
    for copy in copies:
        copy.wait()


def shards(out_grad, hidden_act, inner_params, first_moment, second_moment, anchor, outer_velocity):
    cotangent, act_t = out_grad[0], hidden_act[0].T
    hidden, tokens = act_t.shape
    columns = anchor.shape[1]
    piece = hidden // RING
    bf16, f32 = jnp.bfloat16, jnp.float32
    vmem, dma = pltpu.VMEM, pltpu.SemaphoreType.DMA
    count = ITEMS + 2
    anywhere = pl.BlockSpec(memory_space=pltpu.HBM)
    local = pl.BlockSpec(memory_space=pltpu.VMEM)
    moment, second, new_anchor, new_velocity = pl.pallas_call(
        kernel,
        out_shape=(jax.ShapeDtypeStruct((hidden, columns), f32),) * 4,
        in_specs=[anywhere, local] + [anywhere] * 5,
        out_specs=(local,) * 4,
        scratch_shapes=[
            vmem((2, tokens, cotangent.shape[1] // 2), bf16),
            vmem((sum(BLOCKS), tokens), bf16),
            *[vmem((hidden, columns), f32)] * 5,
            *[vmem((2 if s < 2 else 1, RING, rows, columns), f32) for s, rows in enumerate(BLOCKS)],
            *[vmem((count, 2, rows, LANES), bf16) for count, rows in zip(COUNTS, BLOCKS)] * 2,
            *[vmem((count, 2, 2 * rows, LANES), bf16) for count, rows in zip(COUNTS, BLOCKS)] * 2,
            *[vmem((2 * rows, LANES), bf16) for rows in BLOCKS[:2]] * 2,
            *[vmem((ITEMS, 4 * BLOCKS[2], LANES), bf16)] * 2,
            vmem((2, 8, LANES), f32),
            vmem((10, 8, LANES), f32),
            vmem((RING, piece, LANES), f32),
            vmem((RING, piece, LANES), f32),
            vmem((RING, 2, piece + PAD, LANES), bf16),
            vmem((RING, 2, piece + PAD, LANES), bf16),
            vmem((2, RING, piece, LANES), f32),
            dma((2,)), dma((5,)),
            *[dma((3, count, 2))] * 4,
            dma((2,)), dma((2,)), dma((ITEMS,)), dma((ITEMS,)), dma((10,)), dma((10,)), dma((RING,)), dma((RING,)),
            dma((RING, 2)), dma((RING, 2)), dma((RING,)), dma((RING,)),
        ],
        compiler_params=pltpu.CompilerParams(
            collective_id=0, has_side_effects=True, vmem_limit_bytes=52 * 1024 * 1024),
        cost_estimate=pl.CostEstimate(
            flops=2 * tokens * hidden * cotangent.shape[1], bytes_accessed=12_000_000, transcendentals=8_000_000),
    )(cotangent, act_t, inner_params[0], first_moment[0], second_moment[0], anchor, outer_velocity)
    moment, second, new_anchor, new_velocity = pl.pallas_call(
        place,
        out_shape=(jax.ShapeDtypeStruct((hidden, columns), f32),) * 4,
        in_specs=[local] * 4,
        out_specs=(anywhere,) * 4,
        scratch_shapes=[dma((4,))],
        compiler_params=pltpu.CompilerParams(vmem_limit_bytes=4 * 1024 * 1024),
        cost_estimate=pl.CostEstimate(flops=0, bytes_accessed=32 * hidden * columns, transcendentals=0),
    )(moment, second, new_anchor, new_velocity)
    return (moment[None], second[None], new_anchor, new_velocity)


def solution(mesh):
    return jax.shard_map(
        shards,
        mesh=mesh,
        in_specs=(
            P("replica", "fsdp", None),
            P("replica", "fsdp", None),
            P("replica", None, "fsdp"),
            P("replica", None, "fsdp"),
            P("replica", None, "fsdp"),
            P(None, "fsdp"),
            P(None, "fsdp"),
        ),
        out_specs=(
            P("replica", None, "fsdp"),
            P("replica", None, "fsdp"),
            P(None, "fsdp"),
            P(None, "fsdp"),
        ),
        check_vma=False,
    )
```

```python
import itertools

import jax
import jax.numpy as jnp
from jax import lax
from jax.experimental import pallas as pl
from jax.experimental.pallas import tpu as pltpu
from jax.sharding import PartitionSpec as P

beta_one = 0.9
beta_two = 0.95
inner_rate = 0.1
decay_rate = 0.1
adam_eps = 1e-08
clip_eps = 1e-06
outer_rate = 0.7
outer_mom = 0.9
bias_one = 1.0 - 0.9**50
bias_two = 1.0 - 0.95**50

MESH = pl.DeviceIdType.MESH
LANES = 128
PAD = 16
REACH = 86.0
RING = 4
GROUP = 2 * RING * RING
ITEMS = 8
BLOCKS = (128, 192, 144)
COUNTS = (ITEMS + 2, ITEMS + 2, RING + 1)
ROUND_A, ROUND_B, ROUND_C, EARLY, CROSS = range(5)
SCHEDULE = (
    (0, 0, 0), (0, 1, 0), (3, 2, 0), (0, 0, 7), (0, 0, 2), (3, 2, 4), (0, 1, 4), (0, 0, 1),
    (0, 1, 2), (0, 1, 1), (0, 0, 3), (0, 0, 4), (1, 0, 0), (0, 1, 6), (3, 2, 2), (0, 0, 5),
    (1, 1, 0), (1, 0, 2), (0, 0, 6), (1, 0, 3), (0, 2, 0), (1, 1, 1), (1, 1, 2), (3, 2, 1),
    (0, 1, 3), (1, 0, 4), (2, 0, 0), (2, 1, 0), (3, 2, 6), (0, 1, 8), (0, 2, 2), (0, 1, 5),
    (3, 2, 5), (2, 0, 2), (1, 0, 5), (0, 0, 8), (1, 1, 4), (1, 0, 1), (3, 2, 3), (2, 0, 4),
    (1, 0, 6), (2, 1, 1), (1, 1, 6), (2, 1, 2), (2, 0, 3), (1, 2, 0), (1, 1, 3), (0, 0, 9),
    (0, 2, 1), (3, 2, 7), (1, 1, 8), (0, 2, 3), (2, 0, 1), (1, 0, 8), (2, 1, 4), (0, 1, 7),
    (2, 0, 6), (1, 1, 5), (2, 0, 5), (2, 2, 0), (0, 1, 9), (1, 2, 2), (2, 1, 3), (0, 2, 4),
    (1, 0, 9), (1, 2, 1), (1, 0, 7), (1, 1, 7), (1, 2, 3), (4, 1, 8), (2, 2, 2), (2, 1, 6),
    (2, 1, 5), (1, 1, 9), (2, 2, 1), (1, 2, 4), (4, 0, 8), (2, 0, 7), (2, 0, 9), (2, 2, 3),
    (2, 1, 7), (2, 2, 4), (2, 1, 9),
)


def column_scale(values):
    largest = jnp.max(jnp.abs(values), axis=0, keepdims=True)
    return (largest * 1.01 + 1e-30).astype(jnp.bfloat16).astype(jnp.float32)


def last_line():
    return lax.broadcasted_iota(jnp.int32, (PAD, LANES), 0) == PAD - 1


def encode(message, parts):
    rows = parts[0].shape[0]
    for n, values in enumerate(parts):
        bound = column_scale(values)
        coded = jnp.exp(values * (REACH / bound))
        end = (n + 1) * rows
        message[n * rows : end - PAD, :] = coded[: rows - PAD].astype(jnp.bfloat16)
        message[end - PAD : end, :] = jnp.where(last_line(), bound, coded[rows - PAD :]).astype(jnp.bfloat16)


def decode(message, which, rows):
    block = message[which * rows : (which + 1) * rows, :].astype(jnp.float32)
    values = jnp.log(block) * (block[rows - 1 : rows, :] * (1.0 / REACH))
    return jnp.concatenate([values[: rows - PAD], jnp.where(last_line(), 0.0, values[rows - PAD :])], axis=0)


def kernel(
    cotangent, activations, inner, first, second, anchor, velocity,
    first_out, second_out, anchor_out, velocity_out,
    cot, act_t, inner_v, first_v, second_v, anchor_v, velocity_v,
    partial, other_partial, third_partial,
    send_a0, send_a1, send_a2, recv_a0, recv_a1, recv_a2, send_b0, send_b1, send_b2, recv_b0, recv_b1, recv_b2,
    send_z0, send_z1, recv_z0, recv_z1, send_early, recv_early,
    norm_send, norm_recv, half_send, half_recv, swap_send, swap_recv, pseudo,
    cot_sem, state_sem, sa_sem, ra_sem, sb_sem, rb_sem, sz_sem, rz_sem, se_sem, re_sem,
    ns_sem, nr_sem, hs_sem, hr_sem, ws_sem, wr_sem, ts_sem, tr_sem,
):
    hidden, tokens = activations.shape
    piece = hidden // RING
    width = 2 * LANES
    sums = (partial, other_partial, third_partial)
    send_a, recv_a = (send_a0, send_a1, send_a2), (recv_a0, recv_a1, recv_a2)
    send_b, recv_b = (send_b0, send_b1, send_b2), (recv_b0, recv_b1, recv_b2)
    send_z, recv_z = (send_z0, send_z1), (recv_z0, recv_z1)
    me = lax.axis_index("fsdp")
    rep = lax.axis_index("replica")
    x = me % RING
    y = (me // RING) % RING
    z = me // (RING * RING)
    core = rep % 2
    zh = rep // 2

    def at(px, py, pz):
        return {"fsdp": pz * (RING * RING) + py * RING + px}

    def twin(pzh, pcore):
        return {"replica": pzh * 2 + pcore}

    def along(axis, step):
        if axis == 0:
            return at((x + step) % RING, y, z)
        return at(x, (y + step) % RING, z)

    here = (x, y)
    pair = at(x, y, 1 - z)
    mate = twin(zh, 1 - core)
    partners = (twin(zh + 1 - 2 * (zh % 2), core), twin(RING - 1 - zh, core))
    norm_group = [
        at((x + dx) % RING, (y + dy) % RING, (z + dz) % 2)
        for dx, dy, dz in sorted(
            itertools.product(range(RING), range(RING), range(2)),
            key=lambda d: -min(d[0], RING - d[0]) - min(d[1], RING - d[1]) - d[2])
        if (dx, dy, dz) != (0, 0, 0)
    ]

    halves = cotangent.shape[1] // 2

    def load(k):
        zz = (1 - z) if k == 0 else z
        return pltpu.make_async_copy(
            cotangent.at[:, pl.ds(pl.multiple_of(zz * halves, halves), halves)], cot.at[k], cot_sem.at[k])

    load(0).start()
    load(1).start()
    states = []
    for n, (src, dst) in enumerate((
        (inner, inner_v), (first, first_v), (second, second_v), (anchor, anchor_v), (velocity, velocity_v),
    )):
        states.append(pltpu.make_async_copy(src, dst, state_sem.at[n]))
        states[n].start()

    barrier = pltpu.get_barrier_semaphore()
    everyone = norm_group + [mate, *partners]
    for device in everyone:
        pl.semaphore_signal(barrier, inc=1, device_id=device, device_id_type=MESH)
    def copy_a(s, axis, i, way):
        return pltpu.make_async_remote_copy(
            src_ref=send_a[s].at[i, way], dst_ref=recv_a[s].at[i, way],
            send_sem=sa_sem.at[s, i, way], recv_sem=ra_sem.at[s, i, way],
            device_id=along(axis, 1 if way == 0 else 3), device_id_type=MESH)

    def copy_b(s, axis, i, way):
        return pltpu.make_async_remote_copy(
            src_ref=send_b[s].at[i, way], dst_ref=recv_b[s].at[i, way],
            send_sem=sb_sem.at[s, i, way], recv_sem=rb_sem.at[s, i, way],
            device_id=along(axis, 1 if way == 0 else 3), device_id_type=MESH)

    def copy_z(s):
        return pltpu.make_async_remote_copy(
            src_ref=send_z[s], dst_ref=recv_z[s], send_sem=sz_sem.at[s], recv_sem=rz_sem.at[s],
            device_id=pair, device_id_type=MESH)

    def copy_early(j):
        return pltpu.make_async_remote_copy(
            src_ref=send_early.at[j], dst_ref=recv_early.at[j], send_sem=se_sem.at[j], recv_sem=re_sem.at[j],
            device_id=pair, device_id_type=MESH)

    def offset(i):
        return (2, 1, 3, 0)[i % RING]

    def dot(s, k, chunk):
        columns = pl.ds(pl.multiple_of(chunk * width, width), width)
        first_row, rows = sum(BLOCKS[:s]), BLOCKS[s]
        return jnp.dot(act_t[first_row : first_row + rows, :], cot[k, :, columns], preferred_element_type=jnp.float32)

    def product(s, i, step):
        w = (here[1 - s] + offset(i)) % RING
        t = (here[s] + step) % RING
        return dot(s, i // RING, w * RING + t if s == 0 else t * RING + w)

    def paired(s, n, step):
        order = (2, 1, 3, 0).index(step)
        w = (y + offset(n)) % RING
        t = (x + step) % RING
        j = 2 * n + order // 2
        if order in (0, 2):
            copy_early(j).wait_recv()
        rows = BLOCKS[s]
        arrived = recv_early.at[j]
        both = [decode(arrived, 2 * (order % 2) + h, rows) for h in range(2)]
        return dot(s, 1, w * RING + t) + jnp.concatenate(both, axis=1)

    def summed(s, i, step):
        axis = 1 if s != 1 else 0
        k = i - ITEMS if s < 2 else 0
        return sums[s][k, (here[axis] + step) % RING]

    def fill_a(s, axis, i, own):
        opposite = own(s, i, 2)
        encode(send_a[s].at[i, 0], [opposite[:, :LANES]])
        encode(send_a[s].at[i, 1], [opposite[:, LANES:]])

    def start_a(s, axis, i):
        for way in range(2):
            copy_a(s, axis, i, way).start()

    def round_a(s, axis, i, own):
        fill_a(s, axis, i, own)
        start_a(s, axis, i)

    def round_b(s, axis, i, own):
        rows = BLOCKS[s]
        for way in range(2):
            value = own(s, i, 1 if way == 0 else 3)
            copy_a(s, axis, i, way).wait_recv()
            arrived = decode(recv_a[s].at[i, way], 0, rows)
            left, right = value[:, :LANES], value[:, LANES:]
            if way == 0:
                left = left + arrived
            else:
                right = right + arrived
            encode(send_b[s].at[i, way], [left, right])
            copy_b(s, axis, i, way).start()

    def round_c(s, axis, i, own):
        rows = BLOCKS[s]
        value = own(s, i, 0)
        for way in range(2):
            copy_b(s, axis, i, way).wait_recv()
        parts = []
        for n in range(2):
            parts.append(value[:, n * LANES : (n + 1) * LANES]
                         + decode(recv_b[s].at[i, 0], n, rows) + decode(recv_b[s].at[i, 1], n, rows))
        for way in range(2):
            copy_a(s, axis, i, way).wait_send()
            copy_b(s, axis, i, way).wait_send()
        return parts

    def keep(s, k, w, parts):
        for n in range(2):
            sums[s][k, w, :, n * LANES : (n + 1) * LANES] = parts[n]

    def send_pair(j):
        w = (y + offset(j // 2)) % RING
        parts = []
        for step in ((2, 1), (3, 0))[j % 2]:
            value = dot(2, 0, w * RING + (x + step) % RING)
            parts += [value[:, :LANES], value[:, LANES:]]
        encode(send_early.at[j], parts)
        copy_early(j).start()

    total = jnp.zeros((8, LANES), jnp.float32)
    loaded = False
    spares = []
    ends = (BLOCKS[0], hidden)
    inside = hidden - BLOCKS[0] - BLOCKS[2]
    middle = BLOCKS[0] + inside
    after = BLOCKS[0] + BLOCKS[1]
    line = lax.broadcasted_iota(jnp.int32, (PAD, tokens), 0)
    spare = jnp.zeros((PAD, tokens), jnp.float32)
    for n, (end, place_end) in enumerate(zip(ends, (BLOCKS[0], sum(BLOCKS)))):
        tail_rows = activations[end - PAD : end, :].astype(jnp.float32)
        act_t[place_end - PAD : place_end, :] = jnp.where(line == PAD - 1, 0.0, tail_rows).astype(jnp.bfloat16)
        spare = jnp.where(line == n, tail_rows[PAD - 1 : PAD, :], spare)
    act_t[: BLOCKS[0] - PAD, :] = activations[: BLOCKS[0] - PAD, :]
    act_t[BLOCKS[0] : middle, :] = activations[BLOCKS[0] : middle, :]
    act_t[middle : middle + PAD, :] = spare.astype(jnp.bfloat16)
    act_t[after : sum(BLOCKS) - PAD, :] = activations[middle : hidden - PAD, :]

    load(0).wait()
    for s in range(2):
        fill_a(s, s, 0, product)
    pl.semaphore_wait(barrier, len(everyone))
    for s in range(2):
        start_a(s, s, 0)
    for task, s, i in SCHEDULE[2:]:
        later = i >= COUNTS[s] - (2 if s < 2 else 1)
        axis = (1 if s == 0 else 0) if later and s < 2 else (1 if later or s == 1 else 0)
        own = summed if later else (product if s < 2 else paired)
        if not loaded and not later and task in (ROUND_A, ROUND_B, ROUND_C) and (s == 2 or i >= RING):
            load(1).wait()
            loaded = True
        if task == EARLY:
            send_pair(i)
        elif task == CROSS:
            encode(send_z[s], round_c(s, 1 - s, ITEMS, summed))
            copy_z(s).start()
        elif task == ROUND_A:
            round_a(s, axis, i, own)
        elif task == ROUND_B:
            round_b(s, axis, i, own)
        elif not later:
            keep(s, i // RING, ((here[1 - s] if s < 2 else y) + offset(i)) % RING, round_c(s, axis, i, own))
        elif i == COUNTS[s] - 1:
            rows = BLOCKS[s]
            start, taken = ((0, rows), (BLOCKS[0], inside), (middle, rows))[s]
            parts = round_c(s, axis, i, own)
            if s < 2:
                copy_z(s).wait_recv()
            for n in range(2):
                value = parts[n]
                if s < 2:
                    value = value + decode(recv_z[s], n, rows)
                first_out[start : start + taken, n * LANES : (n + 1) * LANES] = value[:taken]
                if s == 1:
                    spares.append(value[taken : taken + 8])
                total = total + jnp.sum((value * value).reshape(rows // 8, 8, LANES), axis=0)
    for n in range(2):
        for row, end in enumerate(ends):
            first_out[end - 1 : end, n * LANES : (n + 1) * LANES] = spares[n][row : row + 1]
    for state in states:
        state.wait()

    norm_send[...] = total
    sent = [
        pltpu.make_async_remote_copy(
            src_ref=norm_send, dst_ref=norm_recv.at[n], send_sem=ns_sem.at[n], recv_sem=nr_sem.at[n],
            device_id=device, device_id_type=MESH)
        for n, device in enumerate(norm_group)
    ]
    for copy in sent:
        copy.start()
    for copy in sent:
        copy.wait_recv()
    total = total + jnp.sum(norm_recv[...], axis=0)

    mean_square = jnp.sum(total) / (hidden * cotangent.shape[1])
    clip_factor = jnp.minimum(1.0, lax.rsqrt(jnp.full((1, LANES), mean_square + clip_eps, jnp.float32)))

    def difference(part, columns):
        gradient = first_out[part, columns] * clip_factor
        moment = beta_one * first_v[part, columns] + (1.0 - beta_one) * gradient
        square = beta_two * second_v[part, columns] + (1.0 - beta_two) * gradient * gradient
        first_out[part, columns] = moment
        second_out[part, columns] = square
        params = inner_v[part, columns]
        stepped = params - inner_rate * (
            moment / bias_one / (jnp.sqrt(square / bias_two) + adam_eps) + decay_rate * params)
        return anchor_v[part, columns] - stepped

    given = pl.ds(pl.multiple_of((1 - core) * LANES, LANES), LANES)
    kept = pl.ds(pl.multiple_of(core * LANES, LANES), LANES)
    parts = [slice(n * piece, (n + 1) * piece) for n in range(RING)]

    def to_mate(n):
        return pltpu.make_async_remote_copy(
            src_ref=half_send.at[n], dst_ref=half_recv.at[n], send_sem=hs_sem.at[n], recv_sem=hr_sem.at[n],
            device_id=mate, device_id_type=MESH)

    def swap(n, turn):
        return pltpu.make_async_remote_copy(
            src_ref=swap_send.at[n, turn], dst_ref=swap_recv.at[n, turn],
            send_sem=ws_sem.at[n, turn], recv_sem=wr_sem.at[n, turn],
            device_id=partners[(n + turn) % 2], device_id_type=MESH)

    def share(n):
        block = pseudo.at[core, n]
        return pltpu.make_async_remote_copy(
            src_ref=block, dst_ref=block, send_sem=ts_sem.at[n], recv_sem=tr_sem.at[n],
            device_id=mate, device_id_type=MESH)

    def widen(values):
        return jnp.concatenate([values, jnp.zeros((PAD, LANES), jnp.float32)], axis=0)

    for n in range(RING):
        half_send[n] = difference(parts[n], given)
        to_mate(n).start()
    mine = [difference(parts[n], kept) for n in range(RING)]
    for n in range(RING):
        to_mate(n).wait_recv()
        encode(swap_send.at[n, 0], [widen(mine[n] + half_recv[n])])
        swap(n, 0).start()
    for n in range(RING):
        own = decode(swap_send.at[n, 0], 0, piece + PAD)
        swap(n, 0).wait_recv()
        encode(swap_send.at[n, 1], [own + decode(swap_recv.at[n, 0], 0, piece + PAD)])
        swap(n, 1).start()

    def finish(n, which, columns):
        pseudo_grad = pseudo[which, n] / (2 * RING)
        moved = outer_mom * velocity_v[parts[n], columns] + pseudo_grad
        velocity_out[parts[n], columns] = moved
        anchor_out[parts[n], columns] = anchor_v[parts[n], columns] - outer_rate * (pseudo_grad + outer_mom * moved)

    for n in range(RING):
        own = decode(swap_send.at[n, 1], 0, piece + PAD)
        swap(n, 1).wait_recv()
        pseudo[core, n] = (own + decode(swap_recv.at[n, 1], 0, piece + PAD))[:piece]
        share(n).start()
    for n in range(RING):
        finish(n, core, kept)
    for copy in sent + [copy_z(0), copy_z(1), *[to_mate(n) for n in range(RING)]] + [copy_early(j) for j in range(ITEMS)]:
        copy.wait_send()
    for n in range(RING):
        for turn in range(2):
            swap(n, turn).wait_send()
    for n in range(RING):
        share(n).wait_recv()
        finish(n, 1 - core, given)
    for n in range(RING):
        share(n).wait_send()


def place(*refs):
    count = len(refs) // 2
    sems = refs[-1]
    copies = [pltpu.make_async_copy(refs[n], refs[count + n], sems.at[n]) for n in range(count)]
    for copy in copies:
        copy.start()
    for copy in copies:
        copy.wait()


def shards(out_grad, hidden_act, inner_params, first_moment, second_moment, anchor, outer_velocity):
    cotangent, act_t = out_grad[0], hidden_act[0].T
    hidden, tokens = act_t.shape
    columns = anchor.shape[1]
    piece = hidden // RING
    bf16, f32 = jnp.bfloat16, jnp.float32
    vmem, dma = pltpu.VMEM, pltpu.SemaphoreType.DMA
    count = ITEMS + 2
    anywhere = pl.BlockSpec(memory_space=pltpu.HBM)
    local = pl.BlockSpec(memory_space=pltpu.VMEM)
    moment, second, new_anchor, new_velocity = pl.pallas_call(
        kernel,
        out_shape=(jax.ShapeDtypeStruct((hidden, columns), f32),) * 4,
        in_specs=[anywhere, local] + [anywhere] * 5,
        out_specs=(local,) * 4,
        scratch_shapes=[
            vmem((2, tokens, cotangent.shape[1] // 2), bf16),
            vmem((sum(BLOCKS), tokens), bf16),
            *[vmem((hidden, columns), f32)] * 5,
            *[vmem((2 if s < 2 else 1, RING, rows, columns), f32) for s, rows in enumerate(BLOCKS)],
            *[vmem((count, 2, rows, LANES), bf16) for count, rows in zip(COUNTS, BLOCKS)] * 2,
            *[vmem((count, 2, 2 * rows, LANES), bf16) for count, rows in zip(COUNTS, BLOCKS)] * 2,
            *[vmem((2 * rows, LANES), bf16) for rows in BLOCKS[:2]] * 2,
            *[vmem((ITEMS, 4 * BLOCKS[2], LANES), bf16)] * 2,
            vmem((8, LANES), f32),
            vmem((GROUP - 1, 8, LANES), f32),
            vmem((RING, piece, LANES), f32),
            vmem((RING, piece, LANES), f32),
            vmem((RING, 2, piece + PAD, LANES), bf16),
            vmem((RING, 2, piece + PAD, LANES), bf16),
            vmem((2, RING, piece, LANES), f32),
            dma((2,)), dma((5,)),
            *[dma((3, count, 2))] * 4,
            dma((2,)), dma((2,)), dma((ITEMS,)), dma((ITEMS,)), dma((GROUP - 1,)), dma((GROUP - 1,)), dma((RING,)), dma((RING,)),
            dma((RING, 2)), dma((RING, 2)), dma((RING,)), dma((RING,)),
        ],
        compiler_params=pltpu.CompilerParams(
            collective_id=0, has_side_effects=True, vmem_limit_bytes=52 * 1024 * 1024),
        cost_estimate=pl.CostEstimate(
            flops=2 * tokens * hidden * cotangent.shape[1], bytes_accessed=12_000_000, transcendentals=8_000_000),
    )(cotangent, act_t, inner_params[0], first_moment[0], second_moment[0], anchor, outer_velocity)
    moment, second, new_anchor, new_velocity = pl.pallas_call(
        place,
        out_shape=(jax.ShapeDtypeStruct((hidden, columns), f32),) * 4,
        in_specs=[local] * 4,
        out_specs=(anywhere,) * 4,
        scratch_shapes=[dma((4,))],
        compiler_params=pltpu.CompilerParams(vmem_limit_bytes=4 * 1024 * 1024),
        cost_estimate=pl.CostEstimate(flops=0, bytes_accessed=32 * hidden * columns, transcendentals=0),
    )(moment, second, new_anchor, new_velocity)
    return (moment[None], second[None], new_anchor, new_velocity)


def solution(mesh):
    return jax.shard_map(
        shards,
        mesh=mesh,
        in_specs=(
            P("replica", "fsdp", None),
            P("replica", "fsdp", None),
            P("replica", None, "fsdp"),
            P("replica", None, "fsdp"),
            P("replica", None, "fsdp"),
            P(None, "fsdp"),
            P(None, "fsdp"),
        ),
        out_specs=(
            P("replica", None, "fsdp"),
            P("replica", None, "fsdp"),
            P(None, "fsdp"),
            P(None, "fsdp"),
        ),
        check_vma=False,
    )
```
